32 devices in a mesh: seg: 2 (over x), state: 16 (over z, y, core).
Axes of the slice: x: 2, y: 2, z: 4, core: 2. Of those that a mesh axis runs over, the one named last changes fastest.
Arguments:
- forward_in: float32 [2, 8388608], P('seg', 'state'), may hold values from 0.3 to 28, as said below
- backward_in: float32 [2, 8388608], P('seg', 'state'), may hold values from 0.3 to 28, as said below
- compat_masks: int32 [4, 23], P('seg'), may hold values from 1 to 3
- theta_index: int32 [4, 23], P('seg'), may hold values from 0 to 5
Outputs:
- forward_out: float32 [2, 8388608], P('seg', 'state')
- backward_out: float32 [2, 8388608], P('seg', 'state')
- posterior: float32 [2, 8388608], P('seg', 'state')
- log_scales: float32 [2, 2], P(None, 'seg')
The draws below stay inside these ranges and needn't reach their ends.
Inputs may be any that keep to these rules, and one draw needn't show every extreme that they name: `compat_masks`: 1 allows anchor 0 only, 2 anchor 1 only, 3 both. `forward_in`: positive. `backward_in`: positive.
All inputs are finite; a program needn't handle non-finite values.
Results may differ from the reference program's by a relative error of at most 0.00011.
Values sent between devices are 32-bit elements; how exact they have to be, the bound alone decides.
A program may use at most 64 MiB of HBM per device.

```python
import jax
import jax.numpy as jnp
from jax import lax

MEIOSES = 23
STATES = 8388608
SEGS = 2
MARKERS = 4


def message_draw(key, salt):
    stream = jax.random.fold_in(key, salt)
    position = jnp.arange(STATES, dtype=jnp.float32) / STATES
    rising = 10.0 ** position
    noise_part = jax.random.uniform(stream, (SEGS, STATES), jnp.float32, -1.0, 1.0)
    return rising[None, :] * jnp.exp(noise_part)


def draw_forward_in(key, part):
    return message_draw(key, 11)


def draw_backward_in(key, part):
    return message_draw(key, 23)


def plant(values, rng, smallest, high):
    spot = [jax.random.randint(jax.random.fold_in(rng, axis), (), 0, length) for axis, length in enumerate(values.shape)]
    main_axis = values.shape.index(max(values.shape))
    neighbour = spot[:main_axis] + [(spot[main_axis] + 1) % values.shape[main_axis]] + spot[main_axis + 1:]
    return values.at[tuple(spot)].set(smallest).at[tuple(neighbour)].set(high)


def setup_inputs(seed: int = 0) -> dict:
    arg_keys = jax.random.split(jax.random.key(seed), 5)
    forward_in = draw_forward_in(jax.random.fold_in(arg_keys[4], 71), 0)
    backward_in = draw_backward_in(jax.random.fold_in(arg_keys[4], 71), 0)
    compat_masks = plant(jax.random.randint(arg_keys[2], (MARKERS, MEIOSES), 1, 4), jax.random.fold_in(arg_keys[2], 1), 1, 3).astype(jnp.int32)
    theta_index = plant(jax.random.randint(arg_keys[3], (MARKERS, MEIOSES), 0, 6), jax.random.fold_in(arg_keys[3], 1), 0, 5).astype(jnp.int32)
    return {"forward_in": forward_in, "backward_in": backward_in, "compat_masks": compat_masks, "theta_index": theta_index}


PENALTY = 0.5
ERROR_RATE = 0.02
BASE_THETA = 0.01


def theta_table(theta_index):
    return BASE_THETA * 2.0 ** theta_index.astype(jnp.float32)


def kron_matrix(thetas):
    count = thetas.shape[0]
    width = 2 ** count
    row_ids = lax.broadcasted_iota(jnp.int32, (width, width), 0)
    col_ids = lax.broadcasted_iota(jnp.int32, (width, width), 1)
    result = jnp.ones((width, width), jnp.float32)
    for which in range(count):
        agrees = (row_ids // 2 ** which) % 2 == (col_ids // 2 ** which) % 2
        result = result * jnp.where(agrees, 1.0 - thetas[which], thetas[which])
    return result


def mix_all(vector, thetas):
    count = thetas.shape[0]
    offset = 0
    current = vector
    while offset < count:
        width_bits = min(4, count - offset)
        shaped = current.reshape(-1, 2 ** width_bits, 2 ** offset)
        current = jnp.einsum("ij,ojk->oik", kron_matrix(thetas[offset:offset + width_bits]), shaped,
                             precision=lax.Precision.HIGHEST).reshape(-1)
        offset += width_bits
    return current


def emission_full(mask_row):
    count = mask_row.shape[0]
    anchor_zero = jnp.where(mask_row % 2 == 1, 1.0, PENALTY).astype(jnp.float32)
    anchor_one = jnp.where(mask_row // 2 == 1, 1.0, PENALTY).astype(jnp.float32)
    product = jnp.ones((1,), jnp.float32)
    for which in range(count):
        pair = jnp.stack([anchor_zero[which], anchor_one[which]])
        product = (pair[:, None] * product[None, :]).reshape(-1)
    return ERROR_RATE + (1.0 - ERROR_RATE) * product


def reference(forward_in, backward_in, compat_masks, theta_index):
    thetas = theta_table(theta_index)
    segments = forward_in.shape[0]
    per_segment = compat_masks.shape[0] // segments
    forwards = []
    backwards = []
    log_fwd = []
    log_bwd = []
    for segment in range(segments):
        forward = forward_in[segment]
        total_log = jnp.zeros((), jnp.float32)
        for offset in range(per_segment):
            marker = segment * per_segment + offset
            update = emission_full(compat_masks[marker]) * mix_all(forward, thetas[marker])
            scale = jnp.mean(update)
            forward = update / scale
            total_log = total_log + jnp.log(scale)
        forwards.append(forward)
        log_fwd.append(total_log)
        backward = backward_in[segment]
        total_log = jnp.zeros((), jnp.float32)
        for offset in range(per_segment - 1, -1, -1):
            marker = segment * per_segment + offset
            update = mix_all(emission_full(compat_masks[marker]) * backward, thetas[marker])
            scale = jnp.mean(update)
            backward = update / scale
            total_log = total_log + jnp.log(scale)
        backwards.append(backward)
        log_bwd.append(total_log)
    posts = []
    for segment in range(segments):
        if segment == 0:
            left_side = forward_in[0]
        else:
            left_side = forwards[segment - 1]
        product = left_side * backwards[segment]
        posts.append(product / jnp.mean(product))
    log_scales = jnp.stack([jnp.stack(log_fwd), jnp.stack(log_bwd)])
    return jnp.stack(forwards), jnp.stack(backwards), jnp.stack(posts), log_scales
```

```python
import functools

import jax
import jax.numpy as jnp
from jax import lax
from jax.experimental import pallas as pl
from jax.experimental.pallas import tpu as pltpu
from jax.sharding import PartitionSpec as P

PENALTY = 0.5
ERROR_RATE = 0.02
BASE_THETA = 0.01
LANES = 128
TILE = 8
MESH = pl.DeviceIdType.MESH
HIGHEST = lax.Precision.HIGHEST


def bits_of(size):
    return size.bit_length() - 1


def kernel(
    groups,
    segs,
    rows,
    masks,
    index,
    f_hbm,
    b_hbm,
    f_out,
    b_out,
    p_out,
    totals_out,
    f_in,
    b_in,
    f_send,
    f_mid,
    f_back,
    f_last,
    b_send,
    b_mid,
    b_back,
    b_last,
    f_raw,
    b_raw,
    p_raw,
    left,
    lane_mats,
    row_mats,
    tables,
    part_src,
    parts,
    load_sem,
    own_sem,
    out_sem,
    send_sem,
    recv_sem,
    seg_send,
    seg_recv,
    part_send,
    part_recv,
):
    me = lax.axis_index("state")
    seg = lax.axis_index("seg")
    later = lax.rem(seg + 1, segs)
    earlier = lax.rem(seg + segs - 1, segs)
    group_bits = bits_of(groups)
    lane_bits = bits_of(LANES)
    row_bits = bits_of(rows)
    swap_first = lane_bits + row_bits
    high_first = swap_first + group_bits
    half = rows // 2

    def partner(turn):
        odd = lax.rem(turn, 2)
        offset = (1 - odd) * (groups // 2 + lax.div(turn, 2)) + odd * lax.div(turn + 1, 2)
        other = 0
        for bit in range(group_bits):
            mine = lax.div(me, 2**bit)
            its = lax.div(offset, 2**bit)
            other = other + lax.rem(mine + its, 2) * 2**bit
        return other

    def each_partner(body):
        def step(turn, carry):
            body(partner(turn))
            return carry

        lax.fori_loop(0, groups - 1, step, 0)

    load_f = pltpu.make_async_copy(f_hbm, f_in, load_sem.at[0])
    load_b = pltpu.make_async_copy(b_hbm, b_in, load_sem.at[1])
    load_f.start()
    load_b.start()

    barrier = pltpu.get_barrier_semaphore()

    def greet(other):
        pl.semaphore_signal(barrier, inc=1, device_id={"state": other}, device_id_type=MESH)

    each_partner(greet)
    pl.semaphore_signal(barrier, inc=1, device_id={"seg": later}, device_id_type=MESH)
    pl.semaphore_signal(barrier, inc=1, device_id={"seg": earlier}, device_id_type=MESH)

    def theta(marker, bit):
        return lax.shift_left(jnp.int32(1), index[marker, bit]).astype(jnp.float32) * BASE_THETA

    def anchors(marker, bit):
        mask = masks[marker, bit]
        zero = jnp.where(lax.rem(mask, 2) == 1, 1.0, PENALTY).astype(jnp.float32)
        one = jnp.where(lax.div(mask, 2) == 1, 1.0, PENALTY).astype(jnp.float32)
        return zero, one

    def own_factor(marker, first):
        factor = jnp.float32(1.0)
        for bit in range(group_bits):
            zero, one = anchors(marker, first + bit)
            factor = factor * jnp.where(lax.rem(lax.div(me, 2**bit), 2) == 1, one, zero)
        return factor

    def group_factors(marker, first, own):
        factors = [own]
        for bit in range(group_bits):
            zero, one = anchors(marker, first + bit)
            factors = [f * zero for f in factors] + [f * one for f in factors]
        return factors

    def thetas(marker, first):
        return [theta(marker, first + bit) for bit in range(group_bits)]

    def mixed(values, mixing):
        values = list(values)
        for bit, amount in enumerate(mixing):
            for low in range(groups):
                high = low + 2**bit
                if low // 2**bit % 2 == 0:
                    moved = amount * (values[high] - values[low])
                    values[low] = values[low] + moved
                    values[high] = values[high] - moved
        return values

    def emitted(values, table, factors):
        return [
            v * (ERROR_RATE + (1.0 - ERROR_RATE) * (factor * table))
            for v, factor in zip(values, factors)
        ]

    def over_tiles(first, count, body, init):
        def step(which, carry):
            start = pl.multiple_of((first + which) * TILE, TILE)
            return body(pl.ds(start, TILE), carry)

        return lax.fori_loop(0, count, step, init)

    def loaded(ref, where):
        return [ref[group, where, :] for group in range(groups)]

    def stored(ref, where, values):
        for group in range(groups):
            ref[group, where, :] = values[group]

    def wave(number, source, target):
        where = pl.ds(number % 2 * half, half)

        def send(other):
            pltpu.make_async_remote_copy(
                src_ref=source.at[other, where],
                dst_ref=target.at[me, where],
                send_sem=send_sem.at[number],
                recv_sem=recv_sem.at[number],
                device_id={"state": other},
                device_id_type=MESH,
            ).start()

        each_partner(send)

    def wave_wait(number, ref, sems):
        view = ref.at[pl.ds(0, groups - 1), pl.ds(number % 2 * half, half)]
        pltpu.make_async_copy(view, view, sems.at[number]).wait()

    def own_copy(number, source, target):
        return pltpu.make_async_copy(source.at[me], target.at[me], own_sem.at[number])

    def share(which, partial):
        part_src[which] = partial
        parts[which, me] = partial

        def send(other):
            pltpu.make_async_remote_copy(
                src_ref=part_src.at[which],
                dst_ref=parts.at[which, me],
                send_sem=part_send.at[which],
                recv_sem=part_recv.at[which],
                device_id={"state": other},
                device_id_type=MESH,
            ).start()

        each_partner(send)

    def shared(which):
        view = parts.at[which, pl.ds(0, groups - 1)]
        pltpu.make_async_copy(view, view, part_send.at[which]).wait()
        pltpu.make_async_copy(view, view, part_recv.at[which]).wait()
        return jnp.sum(jnp.sum(parts[which], axis=0))

    def kron(marker, first, count):
        width = 2**count
        differs = lax.broadcasted_iota(jnp.int32, (width, width), 0) ^ lax.broadcasted_iota(
            jnp.int32, (width, width), 1
        )
        result = jnp.ones((width, width), jnp.float32)
        for bit in range(count):
            amount = theta(marker, first + bit)
            result = result * jnp.where((differs >> bit) & 1 == 0, 1.0 - amount, amount)
        return result

    def low_table(marker):
        lane = lax.broadcasted_iota(jnp.int32, (rows, LANES), 1)
        row = lax.broadcasted_iota(jnp.int32, (rows, LANES), 0)
        result = jnp.ones((rows, LANES), jnp.float32)
        for bit in range(swap_first):
            zero, one = anchors(marker, bit)
            spot = lane >> bit if bit < lane_bits else row >> (bit - lane_bits)
            result = result * jnp.where(spot & 1 == 1, one, zero)
        return result

    tiles = rows // TILE
    nothing = jnp.zeros((TILE, LANES), jnp.float32)

    load_f.wait()
    first_swap = thetas(0, swap_first)

    def start_forward(where, carry):
        stored(f_send, where, mixed(loaded(f_in, where), first_swap))
        return carry

    over_tiles(0, tiles, start_forward, 0)
    pl.semaphore_wait(barrier, groups + 1)
    wave(0, f_send, f_mid)
    wave(1, f_send, f_mid)
    own_f1 = own_copy(0, f_send, f_mid)
    own_f1.start()

    tables[1] = low_table(1)
    load_b.wait()
    last_swap = thetas(1, swap_first)
    last_factors = group_factors(1, swap_first, own_factor(1, high_first))

    def start_backward(where, carry):
        values = emitted(loaded(b_in, where), tables[1, where, :], last_factors)
        stored(b_send, where, mixed(values, last_swap))
        return carry

    over_tiles(0, tiles, start_backward, 0)
    own_b1 = own_copy(1, b_send, b_mid)
    own_b1.start()
    tables[0] = low_table(0)
    for marker in range(2):
        lane_mats[marker] = kron(marker, 0, lane_bits)
        row_mats[marker] = kron(marker, lane_bits, row_bits)
    high_mix = [thetas(0, high_first), thetas(1, high_first)]
    high_factors = group_factors(0, high_first, own_factor(0, swap_first))

    def low_mix(source, target, marker):
        def step(group, carry):
            part = jnp.dot(
                source[group],
                lane_mats[marker],
                precision=HIGHEST,
                preferred_element_type=jnp.float32,
            )
            target[group] = jnp.dot(
                row_mats[marker], part, precision=HIGHEST, preferred_element_type=jnp.float32
            )
            return carry

        lax.fori_loop(0, groups, step, 0)

    def middle(mid, back, before, after):
        low_mix(mid, mid, before)

        def step(where, total):
            values = mixed(loaded(mid, where), high_mix[before])
            values = emitted(values, tables[0, where, :], high_factors)
            stored(mid, where, mixed(values, high_mix[after]))
            return total + sum(values[1:], values[0])

        total = over_tiles(0, tiles, step, nothing)
        low_mix(mid, back, after)
        return total

    wave_wait(0, f_send, send_sem)
    wave(2, b_send, b_mid)
    wave_wait(1, f_send, send_sem)
    wave(3, b_send, b_mid)
    wave_wait(0, f_mid, recv_sem)
    wave_wait(1, f_mid, recv_sem)
    own_f1.wait()
    middle(f_mid, f_back, 0, 1)
    own_f2 = own_copy(2, f_back, f_last)
    own_f2.start()

    wave_wait(2, b_send, send_sem)
    wave(4, f_back, f_last)
    wave_wait(3, b_send, send_sem)
    wave(5, f_back, f_last)
    wave_wait(2, b_mid, recv_sem)
    wave_wait(3, b_mid, recv_sem)
    own_b1.wait()
    b_total = middle(b_mid, b_back, 1, 0)
    own_b2 = own_copy(3, b_back, b_last)
    own_b2.start()
    share(1, b_total)

    def to_later(part):
        where = pl.ds(part * half, half)
        return pltpu.make_async_remote_copy(
            src_ref=f_raw.at[:, where],
            dst_ref=left.at[:, where],
            send_sem=seg_send.at[part],
            recv_sem=seg_recv.at[part],
            device_id={"seg": later},
            device_id_type=MESH,
        )

    def finish_forward(where, total):
        values = emitted(
            mixed(loaded(f_last, where), last_swap), tables[1, where, :], last_factors
        )
        stored(f_raw, where, values)
        return total + sum(values[1:], values[0])

    def finish_backward(where, total):
        values = mixed(loaded(b_last, where), first_swap)
        stored(b_raw, where, values)
        for group in range(groups):
            beside = jnp.where(seg == 0, f_in[group, where, :], left[group, where, :])
            product = beside * values[group]
            p_raw[group, where, :] = product
            total = total + product
        return total

    own_f2.wait()
    f_total = nothing
    for part in range(2):
        wave_wait(4 + part, f_back, send_sem)
        wave(6 + part, b_back, b_last)
        wave_wait(4 + part, f_last, recv_sem)
        f_total = over_tiles(part * tiles // 2, tiles // 2, finish_forward, f_total)
        to_later(part).start()
    save_f = pltpu.make_async_copy(f_raw, f_out, out_sem.at[0])
    save_f.start()
    share(0, f_total)
    own_b2.wait()
    totals_out[0] = shared(0)
    totals_out[1] = shared(1)

    p_total = nothing
    saves = [save_f]
    for part in range(2):
        where = pl.ds(part * half, half)
        wave_wait(6 + part, b_last, recv_sem)
        to_later(part).wait_recv()
        p_total = over_tiles(part * tiles // 2, tiles // 2, finish_backward, p_total)
        for number, (source, target) in enumerate(((b_raw, b_out), (p_raw, p_out))):
            save = pltpu.make_async_copy(
                source.at[:, where], target.at[:, where], out_sem.at[1 + 2 * part + number]
            )
            if part == 0:
                save.start()
            saves.append(save)
    share(2, p_total)
    for save in saves[3:]:
        save.start()
    for part in range(2):
        wave_wait(6 + part, b_back, send_sem)
        to_later(part).wait_send()
    totals_out[2] = shared(2)
    for save in saves:
        save.wait()


def messages(groups, segs, forward, backward, masks, index):
    rows = forward.shape[0] // (groups * LANES)
    shape = (groups, rows, LANES)
    block = pltpu.VMEM(shape, jnp.float32)
    dma = pltpu.SemaphoreType.DMA
    whole = jax.ShapeDtypeStruct(shape, jnp.float32)
    anywhere = pl.BlockSpec(memory_space=pl.ANY)
    scalars = pl.BlockSpec(memory_space=pltpu.SMEM)
    size = forward.shape[0]
    return pl.pallas_call(
        functools.partial(kernel, groups, segs, rows),
        out_shape=(whole, whole, whole, jax.ShapeDtypeStruct((3,), jnp.float32)),
        in_specs=[scalars, scalars, anywhere, anywhere],
        out_specs=(anywhere, anywhere, anywhere, scalars),
        scratch_shapes=[block] * 14
        + [
            pltpu.VMEM((2, LANES, LANES), jnp.float32),
            pltpu.VMEM((2, rows, rows), jnp.float32),
            pltpu.VMEM((2, rows, LANES), jnp.float32),
            pltpu.VMEM((3, TILE, LANES), jnp.float32),
            pltpu.VMEM((3, groups, TILE, LANES), jnp.float32),
            dma((2,)),
            dma((4,)),
            dma((5,)),
            dma((8,)),
            dma((8,)),
            dma((2,)),
            dma((2,)),
            dma((3,)),
            dma((3,)),
        ],
        compiler_params=pltpu.CompilerParams(
            collective_id=0, has_side_effects=True, vmem_limit_bytes=44 * 1024 * 1024
        ),
        cost_estimate=pl.CostEstimate(
            flops=8 * size * (LANES + rows), bytes_accessed=20 * size, transcendentals=0
        ),
    )(masks, index, forward.reshape(shape), backward.reshape(shape))


def shards(forward_in, backward_in, compat_masks, theta_index):
    groups = lax.axis_size("state")
    segs = lax.axis_size("seg")
    total_states = forward_in.shape[1] * groups
    forward, backward, product, totals = messages(
        groups, segs, forward_in[0], backward_in[0], compat_masks, theta_index
    )
    means = totals / total_states
    outs = [
        (raw * (1.0 / means[which])).reshape(1, -1)
        for which, raw in enumerate((forward, backward, product))
    ]
    return (*outs, jnp.log(means[:2]).reshape(2, 1))


def solution(mesh):
    placed = (P("seg", "state"), P("seg", "state"), P("seg", None), P("seg", None))
    return jax.shard_map(
        shards,
        mesh=mesh,
        in_specs=placed,
        out_specs=(P("seg", "state"), P("seg", "state"), P("seg", "state"), P(None, "seg")),
        check_vma=False,
    )
```

```python
import functools

import jax
import jax.numpy as jnp
from jax import lax
from jax.experimental import pallas as pl
from jax.experimental.pallas import tpu as pltpu
from jax.sharding import PartitionSpec as P

PENALTY = 0.5
ERROR_RATE = 0.02
BASE_THETA = 0.01
LANES = 128
TILE = 8
CHUNKS = 4
DEPTH = 2
MESH = pl.DeviceIdType.MESH


def bits_of(size):
    return size.bit_length() - 1


def kernel(
    groups,
    segs,
    rows,
    masks_hbm,
    index_hbm,
    f_hbm,
    b_hbm,
    f_out,
    b_out,
    p_out,
    means_out,
    masks,
    index,
    f_in,
    b_in,
    f_send,
    f_mid,
    f_back,
    f_last,
    b_send,
    b_mid,
    b_back,
    b_last,
    f_raw,
    b_raw,
    p_raw,
    left,
    f_done,
    lane_mats,
    row_mats,
    tables,
    part_src,
    parts,
    load_sem,
    own_sem,
    out_sem,
    send_sem,
    recv_sem,
    seg_send,
    seg_recv,
    part_send,
    part_recv,
):
    me = lax.axis_index("state")
    seg = lax.axis_index("seg")
    later = lax.rem(seg + 1, segs)
    earlier = lax.rem(seg + segs - 1, segs)
    group_bits = bits_of(groups)
    lane_bits = bits_of(LANES)
    row_bits = bits_of(rows)
    swap_first = lane_bits + row_bits
    high_first = swap_first + group_bits
    chunks = min(CHUNKS, rows // TILE)
    part_rows = rows // chunks
    total_states = groups * groups * rows * LANES

    def partner(turn):
        odd = lax.rem(turn, 2)
        offset = (1 - odd) * (groups // 2 + lax.div(turn, 2)) + odd * lax.div(turn + 1, 2)
        other = 0
        for bit in range(group_bits):
            mine = lax.div(me, 2**bit)
            its = lax.div(offset, 2**bit)
            other = other + lax.rem(mine + its, 2) * 2**bit
        return other

    def each_partner(body):
        def step(turn, carry):
            body(partner(turn))
            return carry

        lax.fori_loop(0, groups - 1, step, 0)

    load_f = pltpu.make_async_copy(f_hbm, f_in, load_sem.at[0])
    load_b = pltpu.make_async_copy(b_hbm, b_in, load_sem.at[1])
    load_index = pltpu.make_async_copy(index_hbm, index, load_sem.at[2])
    load_masks = pltpu.make_async_copy(masks_hbm, masks, load_sem.at[3])
    load_index.start()
    load_f.start()
    load_masks.start()
    load_b.start()

    barrier = pltpu.get_barrier_semaphore()

    def greet(other):
        pl.semaphore_signal(barrier, inc=1, device_id={"state": other}, device_id_type=MESH)

    each_partner(greet)
    pl.semaphore_signal(barrier, inc=1, device_id={"seg": later}, device_id_type=MESH)
    pl.semaphore_signal(barrier, inc=1, device_id={"seg": earlier}, device_id_type=MESH)

    def theta(marker, bit):
        return lax.shift_left(jnp.int32(1), index[marker, bit]).astype(jnp.float32) * BASE_THETA

    def anchors(marker, bit):
        mask = masks[marker, bit]
        zero = jnp.where(lax.rem(mask, 2) == 1, 1.0, PENALTY).astype(jnp.float32)
        one = jnp.where(lax.div(mask, 2) == 1, 1.0, PENALTY).astype(jnp.float32)
        return zero, one

    def own_factor(marker, first):
        factor = jnp.float32(1.0)
        for bit in range(group_bits):
            zero, one = anchors(marker, first + bit)
            factor = factor * jnp.where(lax.rem(lax.div(me, 2**bit), 2) == 1, one, zero)
        return factor

    def group_factors(marker, first, own):
        factors = [own]
        for bit in range(group_bits):
            zero, one = anchors(marker, first + bit)
            factors = [f * zero for f in factors] + [f * one for f in factors]
        return factors

    def thetas(marker, first):
        return [theta(marker, first + bit) for bit in range(group_bits)]

    def mixed(values, mixing):
        values = list(values)
        for bit, amount in enumerate(mixing):
            for low in range(groups):
                high = low + 2**bit
                if low // 2**bit % 2 == 0:
                    moved = amount * (values[high] - values[low])
                    values[low] = values[low] + moved
                    values[high] = values[high] - moved
        return values

    def emitted(values, table, factors):
        return [
            v * (ERROR_RATE + (1.0 - ERROR_RATE) * (factor * table))
            for v, factor in zip(values, factors)
        ]

    def over_tiles(first, count, body, init):
        def step(which, carry):
            start = pl.multiple_of((first + which) * TILE, TILE)
            return body(pl.ds(start, TILE), carry)

        return lax.fori_loop(0, count, step, init)

    def loaded(ref, where):
        return [ref[group, where, :] for group in range(groups)]

    def stored(ref, where, values):
        for group in range(groups):
            ref[group, where, :] = values[group]

    swaps = ((f_send, f_mid), (b_send, b_mid), (f_back, f_last), (b_back, b_last))

    def wave_rows(number):
        return pl.ds(number % chunks * part_rows, part_rows)

    def wave_wait(number, side, sems):
        view = swaps[number // chunks][side].at[pl.ds(0, groups - 1), wave_rows(number)]
        pltpu.make_async_copy(view, view, sems.at[number]).wait()

    def sent(number):
        wave_wait(number, 0, send_sem)

    def arrived(number):
        wave_wait(number, 1, recv_sem)

    def wave(number):
        source, target = swaps[number // chunks]
        where = wave_rows(number)
        if number >= DEPTH:
            sent(number - DEPTH)

        def send(other):
            pltpu.make_async_remote_copy(
                src_ref=source.at[other, where],
                dst_ref=target.at[me, where],
                send_sem=send_sem.at[number],
                recv_sem=recv_sem.at[number],
                device_id={"state": other},
                device_id_type=MESH,
            ).start()

        each_partner(send)

    def own_copy(number, source, target):
        return pltpu.make_async_copy(source.at[me], target.at[me], own_sem.at[number])

    def share(which, partial):
        part_src[which] = partial
        parts[which, me] = partial

        def send(other):
            pltpu.make_async_remote_copy(
                src_ref=part_src.at[which],
                dst_ref=parts.at[which, me],
                send_sem=part_send.at[which],
                recv_sem=part_recv.at[which],
                device_id={"state": other},
                device_id_type=MESH,
            ).start()

        each_partner(send)

    def shared(which):
        view = parts.at[which, pl.ds(0, groups - 1)]
        pltpu.make_async_copy(view, view, part_send.at[which]).wait()
        pltpu.make_async_copy(view, view, part_recv.at[which]).wait()
        return jnp.sum(jnp.sum(parts[which], axis=0)) / total_states

    def kron(marker, first, count):
        width = 2**count
        differs = lax.broadcasted_iota(jnp.int32, (width, width), 0) ^ lax.broadcasted_iota(
            jnp.int32, (width, width), 1
        )
        result = jnp.ones((width, width), jnp.float32)
        for bit in range(count):
            amount = theta(marker, first + bit)
            result = result * jnp.where((differs >> bit) & 1 == 0, 1.0 - amount, amount)
        return result

    def low_table(marker):
        lane = lax.broadcasted_iota(jnp.int32, (rows, LANES), 1)
        row = lax.broadcasted_iota(jnp.int32, (rows, LANES), 0)
        result = jnp.ones((rows, LANES), jnp.float32)
        for bit in range(swap_first):
            zero, one = anchors(marker, bit)
            spot = lane >> bit if bit < lane_bits else row >> (bit - lane_bits)
            result = result * jnp.where(spot & 1 == 1, one, zero)
        return result

    tiles = rows // TILE
    part_tiles = tiles // chunks
    nothing = jnp.zeros((TILE, LANES), jnp.float32)

    load_index.wait()
    first_swap = thetas(0, swap_first)
    load_f.wait()

    def start_forward(where, carry):
        stored(f_send, where, mixed(loaded(f_in, where), first_swap))
        return carry

    for part in range(chunks):
        over_tiles(part * part_tiles, part_tiles, start_forward, 0)
        if part == 0:
            pl.semaphore_wait(barrier, groups + 1)
        if part < DEPTH:
            wave(part)
    own_f1 = own_copy(0, f_send, f_mid)
    own_f1.start()

    load_masks.wait()
    tables[1] = low_table(1)
    load_b.wait()
    last_swap = thetas(1, swap_first)
    last_factors = group_factors(1, swap_first, own_factor(1, high_first))

    def start_backward(where, carry):
        values = emitted(loaded(b_in, where), tables[1, where, :], last_factors)
        stored(b_send, where, mixed(values, last_swap))
        return carry

    over_tiles(0, tiles, start_backward, 0)

    def halves(value):
        main = value.astype(jnp.bfloat16)
        return main, (value - main.astype(jnp.float32)).astype(jnp.bfloat16)

    def product(a, b):
        return jnp.dot(a, b, preferred_element_type=jnp.float32)

    for marker in range(2):
        main, rest = halves(kron(marker, 0, lane_bits))
        lane_mats[marker, :LANES] = main
        lane_mats[marker, LANES : 2 * LANES] = main
        lane_mats[marker, 2 * LANES :] = rest
        main, rest = halves(kron(marker, lane_bits, row_bits))
        row_mats[marker, 0] = main
        row_mats[marker, 1] = rest

    def low_mix(source, target, marker):
        def step(pair, carry):
            for which in range(2):
                group = 2 * pair + which
                main, rest = halves(source[group])
                value = product(
                    jnp.concatenate([main, rest], axis=1), lane_mats[marker, : 2 * LANES]
                ) + product(main, lane_mats[marker, 2 * LANES :])
                main, rest = halves(value)
                both = product(row_mats[marker, 0], jnp.concatenate([main, rest], axis=1))
                target[group] = (
                    both[:, :LANES] + both[:, LANES:] + product(row_mats[marker, 1], main)
                )
            return carry

        lax.fori_loop(0, groups // 2, step, 0)

    low_mix(b_send, b_send, 1)
    own_b1 = own_copy(1, b_send, b_mid)
    own_b1.start()
    tables[0] = low_table(0)
    high_mix = [thetas(0, high_first), thetas(1, high_first)]
    high_factors = group_factors(0, high_first, own_factor(0, swap_first))

    def middle(mid, before, after):
        def step(where, total):
            values = mixed(loaded(mid, where), high_mix[before])
            values = emitted(values, tables[0, where, :], high_factors)
            stored(mid, where, mixed(values, high_mix[after]))
            return total + sum(values[1:], values[0])

        return over_tiles(0, tiles, step, nothing)

    for number in range(DEPTH, chunks + DEPTH):
        wave(number)
    for number in range(chunks):
        arrived(number)
    own_f1.wait()
    low_mix(f_mid, f_mid, 0)
    middle(f_mid, 0, 1)
    low_mix(f_mid, f_back, 1)
    own_f2 = own_copy(2, f_back, f_last)
    own_f2.start()

    for number in range(chunks + DEPTH, 2 * chunks + DEPTH):
        wave(number)
    for number in range(chunks, 2 * chunks):
        arrived(number)
    own_b1.wait()
    b_total = middle(b_mid, 1, 0)
    low_mix(b_mid, b_back, 0)
    own_b2 = own_copy(3, b_back, b_last)
    own_b2.start()
    share(1, b_total)

    def to_later(part):
        where = pl.ds(part * part_rows, part_rows)
        return pltpu.make_async_remote_copy(
            src_ref=f_raw.at[:, where],
            dst_ref=left.at[:, where],
            send_sem=seg_send.at[part],
            recv_sem=seg_recv.at[part],
            device_id={"seg": later},
            device_id_type=MESH,
        )

    def finish_forward(where, total):
        values = emitted(
            mixed(loaded(f_last, where), last_swap), tables[1, where, :], last_factors
        )
        stored(f_raw, where, values)
        return total + sum(values[1:], values[0])

    own_f2.wait()
    f_total = nothing
    for part in range(chunks):
        number = 2 * chunks + part
        if number + DEPTH < 4 * chunks:
            wave(number + DEPTH)
        arrived(number)
        f_total = over_tiles(part * part_tiles, part_tiles, finish_forward, f_total)
        to_later(part).start()
    share(0, f_total)
    own_b2.wait()
    means = [shared(0), shared(1)]
    means_out[0] = means[0]
    means_out[1] = means[1]
    f_scale = jnp.float32(1.0) / means[0]
    b_scale = jnp.float32(1.0) / means[1]

    def scale_forward(where, carry):
        stored(f_done, where, [value * f_scale for value in loaded(f_raw, where)])
        return carry

    def finish_backward(where, total):
        values = mixed(loaded(b_last, where), first_swap)
        for group in range(groups):
            value = values[group] * b_scale
            b_raw[group, where, :] = value
            beside = jnp.where(seg == 0, f_in[group, where, :], left[group, where, :])
            joint = beside * value
            p_raw[group, where, :] = joint
            total = total + joint
        return total

    over_tiles(0, tiles, scale_forward, 0)
    saves = [pltpu.make_async_copy(f_done, f_out, out_sem.at[0])]
    saves[0].start()
    p_total = nothing
    for part in range(chunks):
        where = pl.ds(part * part_rows, part_rows)
        number = 3 * chunks + part
        if number + DEPTH < 4 * chunks:
            wave(number + DEPTH)
        arrived(number)
        to_later(part).wait_recv()
        p_total = over_tiles(part * part_tiles, part_tiles, finish_backward, p_total)
        if part == chunks - 1:
            share(2, p_total)
        for side, (source, target) in enumerate(((b_raw, b_out), (p_raw, p_out))):
            save = pltpu.make_async_copy(
                source.at[:, where], target.at[:, where], out_sem.at[1 + 2 * part + side]
            )
            save.start()
            saves.append(save)
    for number in range(4 * chunks - DEPTH, 4 * chunks):
        sent(number)
    for part in range(chunks):
        to_later(part).wait_send()
    means_out[2] = shared(2)
    for save in saves:
        save.wait()


def write_out(means, f_raw, b_raw, p_raw, f_out, b_out, p_out, logs_out, p_in, in_sem, out_sem):
    rows = p_in.shape[1]
    chunks = min(CHUNKS, rows // TILE)
    part_rows = rows // chunks
    views = [pl.ds(part * part_rows, part_rows) for part in range(chunks)]
    reads = [
        pltpu.make_async_copy(p_raw.at[:, where], p_in.at[:, where], in_sem.at[part])
        for part, where in enumerate(views)
    ]
    for read in reads:
        read.start()
    saves = [
        pltpu.make_async_copy(f_raw, f_out, out_sem.at[chunks]),
        pltpu.make_async_copy(b_raw, b_out, out_sem.at[chunks + 1]),
    ]
    for save in saves:
        save.start()
    scale = jnp.float32(1.0) / means[2]
    for part, where in enumerate(views):
        reads[part].wait()

        def step(tile, carry, part=part):
            start = pl.multiple_of(part * part_rows + tile * TILE, TILE)
            spot = pl.ds(start, TILE)
            p_in[:, spot, :] = p_in[:, spot, :] * scale
            return carry

        lax.fori_loop(0, part_rows // TILE, step, 0)
        save = pltpu.make_async_copy(p_in.at[:, where], p_out.at[:, where], out_sem.at[part])
        save.start()
        saves.append(save)
    which = lax.broadcasted_iota(jnp.int32, (1, 2), 1)
    logs_out[...] = jnp.log(jnp.where(which == 0, means[0], means[1]))
    for save in saves:
        save.wait()


def messages(groups, segs, forward, backward, masks, index):
    rows = forward.shape[0] // (groups * LANES)
    shape = (groups, rows, LANES)
    chunks = min(CHUNKS, rows // TILE)
    block = pltpu.VMEM(shape, jnp.float32)
    dma = pltpu.SemaphoreType.DMA
    whole = jax.ShapeDtypeStruct(shape, jnp.float32)
    anywhere = pl.BlockSpec(memory_space=pl.ANY)
    scalars = pl.BlockSpec(memory_space=pltpu.SMEM)
    hbm = pl.BlockSpec(memory_space=pltpu.HBM)
    size = forward.shape[0]
    *raw, means = pl.pallas_call(
        functools.partial(kernel, groups, segs, rows),
        out_shape=(whole, whole, whole, jax.ShapeDtypeStruct((3,), jnp.float32)),
        in_specs=[hbm] * 4,
        out_specs=(anywhere, anywhere, anywhere, scalars),
        scratch_shapes=[
            pltpu.SMEM(masks.shape, jnp.int32),
            pltpu.SMEM(index.shape, jnp.int32),
        ]
        + [block] * 15
        + [
            pltpu.VMEM((2, 3 * LANES, LANES), jnp.bfloat16),
            pltpu.VMEM((2, 2, rows, rows), jnp.bfloat16),
            pltpu.VMEM((2, rows, LANES), jnp.float32),
            pltpu.VMEM((3, TILE, LANES), jnp.float32),
            pltpu.VMEM((3, groups, TILE, LANES), jnp.float32),
            dma((4,)),
            dma((4,)),
            dma((1 + 2 * chunks,)),
            dma((4 * chunks,)),
            dma((4 * chunks,)),
            dma((chunks,)),
            dma((chunks,)),
            dma((3,)),
            dma((3,)),
        ],
        compiler_params=pltpu.CompilerParams(
            collective_id=0, has_side_effects=True, vmem_limit_bytes=44 * 1024 * 1024
        ),
        cost_estimate=pl.CostEstimate(
            flops=8 * size * (LANES + rows), bytes_accessed=20 * size, transcendentals=0
        ),
    )(masks, index, forward.reshape(shape), backward.reshape(shape))
    *outs, logs = pl.pallas_call(
        write_out,
        out_shape=(whole, whole, whole, jax.ShapeDtypeStruct((1, 2), jnp.float32)),
        in_specs=[scalars] + [anywhere] * 3,
        out_specs=(hbm, hbm, hbm, pl.BlockSpec(memory_space=pltpu.VMEM)),
        scratch_shapes=[block, dma((chunks,)), dma((chunks + 2,))],
        compiler_params=pltpu.CompilerParams(vmem_limit_bytes=8 * 1024 * 1024),
        cost_estimate=pl.CostEstimate(flops=size, bytes_accessed=24 * size, transcendentals=2),
    )(means, *raw)
    return (*(out.reshape(1, -1) for out in outs), logs.reshape(2, 1))


def shards(forward_in, backward_in, compat_masks, theta_index):
    groups = lax.axis_size("state")
    segs = lax.axis_size("seg")
    return messages(groups, segs, forward_in[0], backward_in[0], compat_masks, theta_index)


def solution(mesh):
    placed = (P("seg", "state"), P("seg", "state"), P("seg", None), P("seg", None))
    return jax.shard_map(
        shards,
        mesh=mesh,
        in_specs=placed,
        out_specs=(P("seg", "state"), P("seg", "state"), P("seg", "state"), P(None, "seg")),
        check_vma=False,
    )
```

```python
import functools

import jax
import jax.numpy as jnp
from jax import lax
from jax.experimental import pallas as pl
from jax.experimental.pallas import tpu as pltpu
from jax.sharding import PartitionSpec as P

PENALTY = 0.5
ERROR_RATE = 0.02
BASE_THETA = 0.01
LANES = 128
TILE = 8
CHUNKS = 4
DEPTH = 4
MESH = pl.DeviceIdType.MESH


def bits_of(size):
    return size.bit_length() - 1


def kernel(
    groups,
    segs,
    rows,
    masks_hbm,
    index_hbm,
    f_hbm,
    b_hbm,
    f_out,
    b_out,
    p_out,
    means_out,
    masks,
    index,
    f_in,
    b_in,
    f_send,
    f_mid,
    f_back,
    f_last,
    b_send,
    b_mid,
    b_back,
    b_last,
    f_raw,
    b_raw,
    p_raw,
    left,
    f_done,
    lane_mats,
    row_mats,
    tables,
    part_src,
    parts,
    load_sem,
    own_sem,
    out_sem,
    send_sem,
    recv_sem,
    seg_send,
    seg_recv,
    part_send,
    part_recv,
):
    me = lax.axis_index("state")
    seg = lax.axis_index("seg")
    later = lax.rem(seg + 1, segs)
    earlier = lax.rem(seg + segs - 1, segs)
    group_bits = bits_of(groups)
    lane_bits = bits_of(LANES)
    row_bits = bits_of(rows)
    swap_first = lane_bits + row_bits
    high_first = swap_first + group_bits
    chunks = min(CHUNKS, rows // TILE)
    depth = min(DEPTH, chunks)
    part_rows = rows // chunks
    total_states = groups * groups * rows * LANES

    first_turn = lax.rem(me * (groups // 2 - 1), groups - 1)

    def partner(step):
        turn = lax.rem(first_turn + step, groups - 1)
        odd = lax.rem(turn, 2)
        offset = (1 - odd) * (groups // 2 + lax.div(turn, 2)) + odd * lax.div(turn + 1, 2)
        other = 0
        for bit in range(group_bits):
            mine = lax.div(me, 2**bit)
            its = lax.div(offset, 2**bit)
            other = other + lax.rem(mine + its, 2) * 2**bit
        return other

    def each_partner(body):
        def step(turn, carry):
            body(partner(turn))
            return carry

        lax.fori_loop(0, groups - 1, step, 0)

    load_f = pltpu.make_async_copy(f_hbm, f_in, load_sem.at[0])
    load_b = pltpu.make_async_copy(b_hbm, b_in, load_sem.at[1])
    load_index = pltpu.make_async_copy(index_hbm, index, load_sem.at[2])
    load_masks = pltpu.make_async_copy(masks_hbm, masks, load_sem.at[3])
    load_index.start()
    load_f.start()
    load_masks.start()
    load_b.start()

    barrier = pltpu.get_barrier_semaphore()

    def greet(other):
        pl.semaphore_signal(barrier, inc=1, device_id={"state": other}, device_id_type=MESH)

    each_partner(greet)
    pl.semaphore_signal(barrier, inc=1, device_id={"seg": later}, device_id_type=MESH)
    pl.semaphore_signal(barrier, inc=1, device_id={"seg": earlier}, device_id_type=MESH)

    def theta(marker, bit):
        return lax.shift_left(jnp.int32(1), index[marker, bit]).astype(jnp.float32) * BASE_THETA

    def anchors(marker, bit):
        mask = masks[marker, bit]
        zero = jnp.where(lax.rem(mask, 2) == 1, 1.0, PENALTY).astype(jnp.float32)
        one = jnp.where(lax.div(mask, 2) == 1, 1.0, PENALTY).astype(jnp.float32)
        return zero, one

    def own_factor(marker, first):
        factor = jnp.float32(1.0)
        for bit in range(group_bits):
            zero, one = anchors(marker, first + bit)
            factor = factor * jnp.where(lax.rem(lax.div(me, 2**bit), 2) == 1, one, zero)
        return factor

    def group_factors(marker, first, own):
        factors = [own]
        for bit in range(group_bits):
            zero, one = anchors(marker, first + bit)
            factors = [f * zero for f in factors] + [f * one for f in factors]
        return factors

    def thetas(marker, first):
        return [theta(marker, first + bit) for bit in range(group_bits)]

    def mixed(values, mixing):
        values = list(values)
        for bit, amount in enumerate(mixing):
            for low in range(groups):
                high = low + 2**bit
                if low // 2**bit % 2 == 0:
                    moved = amount * (values[high] - values[low])
                    values[low] = values[low] + moved
                    values[high] = values[high] - moved
        return values

    def emitted(values, table, factors):
        return [
            v * (ERROR_RATE + (1.0 - ERROR_RATE) * (factor * table))
            for v, factor in zip(values, factors)
        ]

    def over_tiles(first, count, body, init):
        def step(which, carry):
            start = pl.multiple_of((first + which) * TILE, TILE)
            return body(pl.ds(start, TILE), carry)

        return lax.fori_loop(0, count, step, init)

    def loaded(ref, where):
        return [ref[group, where, :] for group in range(groups)]

    def stored(ref, where, values):
        for group in range(groups):
            ref[group, where, :] = values[group]

    swaps = ((f_send, f_mid), (b_send, b_mid), (f_back, f_last), (b_back, b_last))

    def wave_rows(number):
        return pl.ds(number % chunks * part_rows, part_rows)

    def wave_wait(number, side, sems):
        view = swaps[number // chunks][side].at[pl.ds(0, groups - 1), wave_rows(number)]
        pltpu.make_async_copy(view, view, sems.at[number]).wait()

    def sent(number):
        wave_wait(number, 0, send_sem)

    def arrived(number):
        wave_wait(number, 1, recv_sem)

    def wave(number):
        source, target = swaps[number // chunks]
        where = wave_rows(number)
        if number >= depth:
            sent(number - depth)

        def send(other):
            pltpu.make_async_remote_copy(
                src_ref=source.at[other, where],
                dst_ref=target.at[me, where],
                send_sem=send_sem.at[number],
                recv_sem=recv_sem.at[number],
                device_id={"state": other},
                device_id_type=MESH,
            ).start()

        each_partner(send)

    def own_copy(number, source, target):
        return pltpu.make_async_copy(source.at[me], target.at[me], own_sem.at[number])

    def share(which, partial):
        part_src[which] = partial
        parts[which, me] = partial

        def send(other):
            pltpu.make_async_remote_copy(
                src_ref=part_src.at[which],
                dst_ref=parts.at[which, me],
                send_sem=part_send.at[which],
                recv_sem=part_recv.at[which],
                device_id={"state": other},
                device_id_type=MESH,
            ).start()

        each_partner(send)

    def shared(which):
        view = parts.at[which, pl.ds(0, groups - 1)]
        pltpu.make_async_copy(view, view, part_send.at[which]).wait()
        pltpu.make_async_copy(view, view, part_recv.at[which]).wait()
        return jnp.sum(jnp.sum(parts[which], axis=0)) / total_states

    def kron(marker, first, count):
        width = 2**count
        differs = lax.broadcasted_iota(jnp.int32, (width, width), 0) ^ lax.broadcasted_iota(
            jnp.int32, (width, width), 1
        )
        result = jnp.ones((width, width), jnp.float32)
        for bit in range(count):
            amount = theta(marker, first + bit)
            result = result * jnp.where((differs >> bit) & 1 == 0, 1.0 - amount, amount)
        return result

    def low_table(marker):
        lane = lax.broadcasted_iota(jnp.int32, (rows, LANES), 1)
        row = lax.broadcasted_iota(jnp.int32, (rows, LANES), 0)
        result = jnp.ones((rows, LANES), jnp.float32)
        for bit in range(swap_first):
            zero, one = anchors(marker, bit)
            spot = lane >> bit if bit < lane_bits else row >> (bit - lane_bits)
            result = result * jnp.where(spot & 1 == 1, one, zero)
        return result

    tiles = rows // TILE
    part_tiles = tiles // chunks
    nothing = jnp.zeros((TILE, LANES), jnp.float32)

    load_index.wait()
    first_swap = thetas(0, swap_first)
    load_f.wait()

    def start_forward(where, carry):
        stored(f_send, where, mixed(loaded(f_in, where), first_swap))
        return carry

    for part in range(chunks):
        over_tiles(part * part_tiles, part_tiles, start_forward, 0)
        if part == 0:
            pl.semaphore_wait(barrier, groups + 1)
        if part < depth:
            wave(part)
    own_f1 = own_copy(0, f_send, f_mid)
    own_f1.start()

    load_masks.wait()
    tables[1] = low_table(1)
    load_b.wait()
    last_swap = thetas(1, swap_first)
    last_factors = group_factors(1, swap_first, own_factor(1, high_first))

    def start_backward(where, carry):
        values = emitted(loaded(b_in, where), tables[1, where, :], last_factors)
        stored(b_send, where, mixed(values, last_swap))
        return carry

    over_tiles(0, tiles, start_backward, 0)

    def halves(value):
        main = value.astype(jnp.bfloat16)
        return main, (value - main.astype(jnp.float32)).astype(jnp.bfloat16)

    def product(a, b):
        return jnp.dot(a, b, preferred_element_type=jnp.float32)

    for marker in range(2):
        main, rest = halves(kron(marker, 0, lane_bits))
        lane_mats[marker, :LANES] = main
        lane_mats[marker, LANES : 2 * LANES] = main
        lane_mats[marker, 2 * LANES :] = rest
        main, rest = halves(kron(marker, lane_bits, row_bits))
        row_mats[marker, 0] = main
        row_mats[marker, 1] = rest

    def low_mix(source, target, marker):
        def step(pair, carry):
            for which in range(2):
                group = 2 * pair + which
                main, rest = halves(source[group])
                value = product(
                    jnp.concatenate([main, rest], axis=1), lane_mats[marker, : 2 * LANES]
                ) + product(main, lane_mats[marker, 2 * LANES :])
                main, rest = halves(value)
                both = product(row_mats[marker, 0], jnp.concatenate([main, rest], axis=1))
                target[group] = (
                    both[:, :LANES] + both[:, LANES:] + product(row_mats[marker, 1], main)
                )
            return carry

        lax.fori_loop(0, groups // 2, step, 0)

    low_mix(b_send, b_send, 1)
    own_b1 = own_copy(1, b_send, b_mid)
    own_b1.start()
    tables[0] = low_table(0)
    high_mix = [thetas(0, high_first), thetas(1, high_first)]
    high_factors = group_factors(0, high_first, own_factor(0, swap_first))

    def middle(mid, before, after):
        def step(where, total):
            values = mixed(loaded(mid, where), high_mix[before])
            values = emitted(values, tables[0, where, :], high_factors)
            stored(mid, where, mixed(values, high_mix[after]))
            return total + sum(values[1:], values[0])

        return over_tiles(0, tiles, step, nothing)

    for number in range(depth, chunks + depth):
        wave(number)
    for number in range(chunks):
        arrived(number)
    own_f1.wait()
    low_mix(f_mid, f_mid, 0)
    middle(f_mid, 0, 1)
    low_mix(f_mid, f_back, 1)
    own_f2 = own_copy(2, f_back, f_last)
    own_f2.start()

    for number in range(chunks + depth, 2 * chunks + depth):
        wave(number)
    for number in range(chunks, 2 * chunks):
        arrived(number)
    own_b1.wait()
    b_total = middle(b_mid, 1, 0)
    low_mix(b_mid, b_back, 0)
    own_b2 = own_copy(3, b_back, b_last)
    own_b2.start()
    share(1, b_total)

    def to_later(part):
        where = pl.ds(part * part_rows, part_rows)
        return pltpu.make_async_remote_copy(
            src_ref=f_raw.at[:, where],
            dst_ref=left.at[:, where],
            send_sem=seg_send.at[part],
            recv_sem=seg_recv.at[part],
            device_id={"seg": later},
            device_id_type=MESH,
        )

    def finish_forward(where, total):
        values = emitted(
            mixed(loaded(f_last, where), last_swap), tables[1, where, :], last_factors
        )
        stored(f_raw, where, values)
        return total + sum(values[1:], values[0])

    own_f2.wait()
    f_total = nothing
    for part in range(chunks):
        number = 2 * chunks + part
        if number + depth < 4 * chunks:
            wave(number + depth)
        arrived(number)
        f_total = over_tiles(part * part_tiles, part_tiles, finish_forward, f_total)
        to_later(part).start()
    share(0, f_total)
    own_b2.wait()
    means = [shared(0), shared(1)]
    means_out[0] = means[0]
    means_out[1] = means[1]
    f_scale = jnp.float32(1.0) / means[0]
    b_scale = jnp.float32(1.0) / means[1]

    def scale_forward(where, carry):
        stored(f_done, where, [value * f_scale for value in loaded(f_raw, where)])
        return carry

    def finish_backward(where, total):
        values = mixed(loaded(b_last, where), first_swap)
        for group in range(groups):
            value = values[group] * b_scale
            b_raw[group, where, :] = value
            beside = jnp.where(seg == 0, f_in[group, where, :], left[group, where, :])
            joint = beside * value
            p_raw[group, where, :] = joint
            total = total + joint
        return total

    over_tiles(0, tiles, scale_forward, 0)
    saves = [pltpu.make_async_copy(f_done, f_out, out_sem.at[0])]
    saves[0].start()
    p_total = nothing
    for part in range(chunks):
        where = pl.ds(part * part_rows, part_rows)
        number = 3 * chunks + part
        if number + depth < 4 * chunks:
            wave(number + depth)
        arrived(number)
        to_later(part).wait_recv()
        p_total = over_tiles(part * part_tiles, part_tiles, finish_backward, p_total)
        if part == chunks - 1:
            share(2, p_total)
        for side, (source, target) in enumerate(((b_raw, b_out), (p_raw, p_out))):
            save = pltpu.make_async_copy(
                source.at[:, where], target.at[:, where], out_sem.at[1 + 2 * part + side]
            )
            save.start()
            saves.append(save)
    for number in range(4 * chunks - depth, 4 * chunks):
        sent(number)
    for part in range(chunks):
        to_later(part).wait_send()
    means_out[2] = shared(2)
    for save in saves:
        save.wait()


def write_out(means, f_raw, b_raw, p_raw, f_out, b_out, p_out, logs_out, p_in, in_sem, out_sem):
    rows = p_in.shape[1]
    chunks = min(CHUNKS, rows // TILE)
    part_rows = rows // chunks
    views = [pl.ds(part * part_rows, part_rows) for part in range(chunks)]
    reads = [
        pltpu.make_async_copy(p_raw.at[:, where], p_in.at[:, where], in_sem.at[part])
        for part, where in enumerate(views)
    ]
    for read in reads:
        read.start()
    saves = [
        pltpu.make_async_copy(f_raw, f_out, out_sem.at[chunks]),
        pltpu.make_async_copy(b_raw, b_out, out_sem.at[chunks + 1]),
    ]
    for save in saves:
        save.start()
    scale = jnp.float32(1.0) / means[2]
    for part, where in enumerate(views):
        reads[part].wait()

        def step(tile, carry, part=part):
            start = pl.multiple_of(part * part_rows + tile * TILE, TILE)
            spot = pl.ds(start, TILE)
            p_in[:, spot, :] = p_in[:, spot, :] * scale
            return carry

        lax.fori_loop(0, part_rows // TILE, step, 0)
        save = pltpu.make_async_copy(p_in.at[:, where], p_out.at[:, where], out_sem.at[part])
        save.start()
        saves.append(save)
    which = lax.broadcasted_iota(jnp.int32, (1, 2), 1)
    logs_out[...] = jnp.log(jnp.where(which == 0, means[0], means[1]))
    for save in saves:
        save.wait()


def messages(groups, segs, forward, backward, masks, index):
    rows = forward.shape[0] // (groups * LANES)
    shape = (groups, rows, LANES)
    chunks = min(CHUNKS, rows // TILE)
    block = pltpu.VMEM(shape, jnp.float32)
    dma = pltpu.SemaphoreType.DMA
    whole = jax.ShapeDtypeStruct(shape, jnp.float32)
    anywhere = pl.BlockSpec(memory_space=pl.ANY)
    scalars = pl.BlockSpec(memory_space=pltpu.SMEM)
    hbm = pl.BlockSpec(memory_space=pltpu.HBM)
    size = forward.shape[0]
    *raw, means = pl.pallas_call(
        functools.partial(kernel, groups, segs, rows),
        out_shape=(whole, whole, whole, jax.ShapeDtypeStruct((3,), jnp.float32)),
        in_specs=[hbm] * 4,
        out_specs=(anywhere, anywhere, anywhere, scalars),
        scratch_shapes=[
            pltpu.SMEM(masks.shape, jnp.int32),
            pltpu.SMEM(index.shape, jnp.int32),
        ]
        + [block] * 15
        + [
            pltpu.VMEM((2, 3 * LANES, LANES), jnp.bfloat16),
            pltpu.VMEM((2, 2, rows, rows), jnp.bfloat16),
            pltpu.VMEM((2, rows, LANES), jnp.float32),
            pltpu.VMEM((3, TILE, LANES), jnp.float32),
            pltpu.VMEM((3, groups, TILE, LANES), jnp.float32),
            dma((4,)),
            dma((4,)),
            dma((1 + 2 * chunks,)),
            dma((4 * chunks,)),
            dma((4 * chunks,)),
            dma((chunks,)),
            dma((chunks,)),
            dma((3,)),
            dma((3,)),
        ],
        compiler_params=pltpu.CompilerParams(
            collective_id=0, has_side_effects=True, vmem_limit_bytes=44 * 1024 * 1024
        ),
        cost_estimate=pl.CostEstimate(
            flops=8 * size * (LANES + rows), bytes_accessed=20 * size, transcendentals=0
        ),
    )(masks, index, forward.reshape(shape), backward.reshape(shape))
    *outs, logs = pl.pallas_call(
        write_out,
        out_shape=(whole, whole, whole, jax.ShapeDtypeStruct((1, 2), jnp.float32)),
        in_specs=[scalars] + [anywhere] * 3,
        out_specs=(hbm, hbm, hbm, pl.BlockSpec(memory_space=pltpu.VMEM)),
        scratch_shapes=[block, dma((chunks,)), dma((chunks + 2,))],
        compiler_params=pltpu.CompilerParams(vmem_limit_bytes=8 * 1024 * 1024),
        cost_estimate=pl.CostEstimate(flops=size, bytes_accessed=24 * size, transcendentals=2),
    )(means, *raw)
    return (*(out.reshape(1, -1) for out in outs), logs.reshape(2, 1))


def shards(forward_in, backward_in, compat_masks, theta_index):
    groups = lax.axis_size("state")
    segs = lax.axis_size("seg")
    return messages(groups, segs, forward_in[0], backward_in[0], compat_masks, theta_index)


def solution(mesh):
    placed = (P("seg", "state"), P("seg", "state"), P("seg", None), P("seg", None))
    return jax.shard_map(
        shards,
        mesh=mesh,
        in_specs=placed,
        out_specs=(P("seg", "state"), P("seg", "state"), P("seg", "state"), P(None, "seg")),
        check_vma=False,
    )
```

```python
import functools

import jax
import jax.numpy as jnp
from jax import lax
from jax.experimental import pallas as pl
from jax.experimental.pallas import tpu as pltpu
from jax.sharding import PartitionSpec as P

PENALTY = 0.5
ERROR_RATE = 0.02
BASE_THETA = 0.01
LANES = 128
TILE = 8
CHUNKS = 4
DEPTH = 3
MESH = pl.DeviceIdType.MESH


def bits_of(size):
    return size.bit_length() - 1


def kernel(
    groups,
    segs,
    rows,
    masks_hbm,
    index_hbm,
    f_hbm,
    b_hbm,
    f_out,
    b_out,
    p_out,
    means_out,
    masks,
    index,
    f_in,
    b_in,
    f_send,
    f_mid,
    f_back,
    f_last,
    b_send,
    b_mid,
    b_back,
    b_last,
    f_raw,
    b_raw,
    p_raw,
    left,
    f_done,
    lane_mats,
    row_mats,
    tables,
    part_src,
    parts,
    load_sem,
    own_sem,
    out_sem,
    send_sem,
    recv_sem,
    seg_send,
    seg_recv,
    part_send,
    part_recv,
):
    me = lax.axis_index("state")
    seg = lax.axis_index("seg")
    later = lax.rem(seg + 1, segs)
    earlier = lax.rem(seg + segs - 1, segs)
    group_bits = bits_of(groups)
    lane_bits = bits_of(LANES)
    row_bits = bits_of(rows)
    swap_first = lane_bits + row_bits
    high_first = swap_first + group_bits
    chunks = min(CHUNKS, rows // TILE)
    depth = min(DEPTH, chunks)
    part_rows = rows // chunks
    total_states = groups * groups * rows * LANES

    first_turn = lax.rem(me * (groups // 2 - 1), groups - 1)

    def partner(step):
        turn = lax.rem(first_turn + step, groups - 1)
        odd = lax.rem(turn, 2)
        offset = (1 - odd) * (groups // 2 + lax.div(turn, 2)) + odd * lax.div(turn + 1, 2)
        other = 0
        for bit in range(group_bits):
            mine = lax.div(me, 2**bit)
            its = lax.div(offset, 2**bit)
            other = other + lax.rem(mine + its, 2) * 2**bit
        return other

    def each_partner(body):
        def step(turn, carry):
            body(partner(turn))
            return carry

        lax.fori_loop(0, groups - 1, step, 0)

    load_f = pltpu.make_async_copy(f_hbm, f_in, load_sem.at[0])
    load_b = pltpu.make_async_copy(b_hbm, b_in, load_sem.at[1])
    load_index = pltpu.make_async_copy(index_hbm, index, load_sem.at[2])
    load_masks = pltpu.make_async_copy(masks_hbm, masks, load_sem.at[3])
    load_index.start()
    load_f.start()
    load_masks.start()
    load_b.start()

    barrier = pltpu.get_barrier_semaphore()

    def greet(other):
        pl.semaphore_signal(barrier, inc=1, device_id={"state": other}, device_id_type=MESH)

    each_partner(greet)
    pl.semaphore_signal(barrier, inc=1, device_id={"seg": later}, device_id_type=MESH)
    pl.semaphore_signal(barrier, inc=1, device_id={"seg": earlier}, device_id_type=MESH)

    def theta(marker, bit):
        return lax.shift_left(jnp.int32(1), index[marker, bit]).astype(jnp.float32) * BASE_THETA

    def anchors(marker, bit):
        mask = masks[marker, bit]
        zero = jnp.where(lax.rem(mask, 2) == 1, 1.0, PENALTY).astype(jnp.float32)
        one = jnp.where(lax.div(mask, 2) == 1, 1.0, PENALTY).astype(jnp.float32)
        return zero, one

    def own_factor(marker, first):
        factor = jnp.float32(1.0)
        for bit in range(group_bits):
            zero, one = anchors(marker, first + bit)
            factor = factor * jnp.where(lax.rem(lax.div(me, 2**bit), 2) == 1, one, zero)
        return factor

    def group_factors(marker, first, own):
        factors = [own]
        for bit in range(group_bits):
            zero, one = anchors(marker, first + bit)
            factors = [f * zero for f in factors] + [f * one for f in factors]
        return factors

    def thetas(marker, first):
        return [theta(marker, first + bit) for bit in range(group_bits)]

    def mixed(values, mixing):
        values = list(values)
        for bit, amount in enumerate(mixing):
            for low in range(groups):
                high = low + 2**bit
                if low // 2**bit % 2 == 0:
                    moved = amount * (values[high] - values[low])
                    values[low] = values[low] + moved
                    values[high] = values[high] - moved
        return values

    def emitted(values, table, factors):
        return [
            v * (ERROR_RATE + (1.0 - ERROR_RATE) * (factor * table))
            for v, factor in zip(values, factors)
        ]

    def over_tiles(first, count, body, init):
        def step(which, carry):
            start = pl.multiple_of((first + which) * TILE, TILE)
            return body(pl.ds(start, TILE), carry)

        return lax.fori_loop(0, count, step, init)

    def loaded(ref, where):
        return [ref[group, where, :] for group in range(groups)]

    def stored(ref, where, values):
        for group in range(groups):
            ref[group, where, :] = values[group]

    swaps = ((f_send, f_mid), (b_send, b_mid), (f_back, f_last), (b_back, b_last))

    def wave_rows(number):
        return pl.ds(number % chunks * part_rows, part_rows)

    def wave_wait(number, side, sems):
        view = swaps[number // chunks][side].at[pl.ds(0, groups - 1), wave_rows(number)]
        pltpu.make_async_copy(view, view, sems.at[number]).wait()

    def sent(number):
        wave_wait(number, 0, send_sem)

    here = set()

    def arrived(number):
        if number not in here:
            here.add(number)
            wave_wait(number, 1, recv_sem)

    def wave(number):
        source, target = swaps[number // chunks]
        where = wave_rows(number)
        if number >= depth:
            sent(number - depth)
            arrived(number - depth)

        def send(other):
            pltpu.make_async_remote_copy(
                src_ref=source.at[other, where],
                dst_ref=target.at[me, where],
                send_sem=send_sem.at[number],
                recv_sem=recv_sem.at[number],
                device_id={"state": other},
                device_id_type=MESH,
            ).start()

        each_partner(send)

    def own_copy(number, source, target):
        return pltpu.make_async_copy(source.at[me], target.at[me], own_sem.at[number])

    def share(which, partial):
        part_src[which] = partial
        parts[which, me] = partial

        def send(other):
            pltpu.make_async_remote_copy(
                src_ref=part_src.at[which],
                dst_ref=parts.at[which, me],
                send_sem=part_send.at[which],
                recv_sem=part_recv.at[which],
                device_id={"state": other},
                device_id_type=MESH,
            ).start()

        each_partner(send)

    def shared(which):
        view = parts.at[which, pl.ds(0, groups - 1)]
        pltpu.make_async_copy(view, view, part_send.at[which]).wait()
        pltpu.make_async_copy(view, view, part_recv.at[which]).wait()
        return jnp.sum(jnp.sum(parts[which], axis=0)) / total_states

    def kron(marker, first, count):
        width = 2**count
        differs = lax.broadcasted_iota(jnp.int32, (width, width), 0) ^ lax.broadcasted_iota(
            jnp.int32, (width, width), 1
        )
        result = jnp.ones((width, width), jnp.float32)
        for bit in range(count):
            amount = theta(marker, first + bit)
            result = result * jnp.where((differs >> bit) & 1 == 0, 1.0 - amount, amount)
        return result

    def low_table(marker):
        lane = lax.broadcasted_iota(jnp.int32, (rows, LANES), 1)
        row = lax.broadcasted_iota(jnp.int32, (rows, LANES), 0)
        result = jnp.ones((rows, LANES), jnp.float32)
        for bit in range(swap_first):
            zero, one = anchors(marker, bit)
            spot = lane >> bit if bit < lane_bits else row >> (bit - lane_bits)
            result = result * jnp.where(spot & 1 == 1, one, zero)
        return result

    tiles = rows // TILE
    part_tiles = tiles // chunks
    nothing = jnp.zeros((TILE, LANES), jnp.float32)

    load_index.wait()
    first_swap = thetas(0, swap_first)
    load_f.wait()

    def start_forward(where, carry):
        stored(f_send, where, mixed(loaded(f_in, where), first_swap))
        return carry

    for part in range(chunks):
        over_tiles(part * part_tiles, part_tiles, start_forward, 0)
        if part == 0:
            pl.semaphore_wait(barrier, groups + 1)
        if part < depth:
            wave(part)
    own_f1 = own_copy(0, f_send, f_mid)
    own_f1.start()

    load_masks.wait()
    tables[1] = low_table(1)
    load_b.wait()
    last_swap = thetas(1, swap_first)
    last_factors = group_factors(1, swap_first, own_factor(1, high_first))

    def start_backward(where, carry):
        values = emitted(loaded(b_in, where), tables[1, where, :], last_factors)
        stored(b_send, where, mixed(values, last_swap))
        return carry

    over_tiles(0, tiles, start_backward, 0)

    def halves(value):
        main = value.astype(jnp.bfloat16)
        return main, (value - main.astype(jnp.float32)).astype(jnp.bfloat16)

    def product(a, b):
        return jnp.dot(a, b, preferred_element_type=jnp.float32)

    for marker in range(2):
        main, rest = halves(kron(marker, 0, lane_bits))
        lane_mats[marker, :LANES] = main
        lane_mats[marker, LANES : 2 * LANES] = main
        lane_mats[marker, 2 * LANES :] = rest
        main, rest = halves(kron(marker, lane_bits, row_bits))
        row_mats[marker, 0] = main
        row_mats[marker, 1] = rest

    def low_mix(source, target, marker):
        def step(pair, carry):
            for which in range(2):
                group = 2 * pair + which
                main, rest = halves(source[group])
                value = product(
                    jnp.concatenate([main, rest], axis=1), lane_mats[marker, : 2 * LANES]
                ) + product(main, lane_mats[marker, 2 * LANES :])
                main, rest = halves(value)
                both = product(row_mats[marker, 0], jnp.concatenate([main, rest], axis=1))
                target[group] = (
                    both[:, :LANES] + both[:, LANES:] + product(row_mats[marker, 1], main)
                )
            return carry

        lax.fori_loop(0, groups // 2, step, 0)

    low_mix(b_send, b_send, 1)
    own_b1 = own_copy(1, b_send, b_mid)
    own_b1.start()
    tables[0] = low_table(0)
    high_mix = [thetas(0, high_first), thetas(1, high_first)]
    high_factors = group_factors(0, high_first, own_factor(0, swap_first))

    def middle(mid, before, after):
        def step(where, total):
            values = mixed(loaded(mid, where), high_mix[before])
            values = emitted(values, tables[0, where, :], high_factors)
            stored(mid, where, mixed(values, high_mix[after]))
            return total + sum(values[1:], values[0])

        return over_tiles(0, tiles, step, nothing)

    for number in range(depth, chunks + depth):
        wave(number)
    for number in range(chunks):
        arrived(number)
    own_f1.wait()
    low_mix(f_mid, f_mid, 0)
    middle(f_mid, 0, 1)
    low_mix(f_mid, f_back, 1)
    own_f2 = own_copy(2, f_back, f_last)
    own_f2.start()

    for number in range(chunks + depth, 2 * chunks + depth):
        wave(number)
    for number in range(chunks, 2 * chunks):
        arrived(number)
    own_b1.wait()
    b_total = middle(b_mid, 1, 0)
    low_mix(b_mid, b_back, 0)
    own_b2 = own_copy(3, b_back, b_last)
    own_b2.start()
    share(1, b_total)

    def to_later(part):
        where = pl.ds(part * part_rows, part_rows)
        return pltpu.make_async_remote_copy(
            src_ref=f_raw.at[:, where],
            dst_ref=left.at[:, where],
            send_sem=seg_send.at[part],
            recv_sem=seg_recv.at[part],
            device_id={"seg": later},
            device_id_type=MESH,
        )

    def finish_forward(where, total):
        values = emitted(
            mixed(loaded(f_last, where), last_swap), tables[1, where, :], last_factors
        )
        stored(f_raw, where, values)
        return total + sum(values[1:], values[0])

    own_f2.wait()
    f_total = nothing
    for part in range(chunks):
        number = 2 * chunks + part
        if number + depth < 4 * chunks:
            wave(number + depth)
        arrived(number)
        f_total = over_tiles(part * part_tiles, part_tiles, finish_forward, f_total)
        to_later(part).start()
    share(0, f_total)
    own_b2.wait()
    means = [shared(0), shared(1)]
    means_out[0] = means[0]
    means_out[1] = means[1]
    f_scale = jnp.float32(1.0) / means[0]
    b_scale = jnp.float32(1.0) / means[1]

    def scale_forward(where, carry):
        stored(f_done, where, [value * f_scale for value in loaded(f_raw, where)])
        return carry

    def finish_backward(where, total):
        values = mixed(loaded(b_last, where), first_swap)
        for group in range(groups):
            value = values[group] * b_scale
            b_raw[group, where, :] = value
            beside = jnp.where(seg == 0, f_in[group, where, :], left[group, where, :])
            joint = beside * value
            p_raw[group, where, :] = joint
            total = total + joint
        return total

    over_tiles(0, tiles, scale_forward, 0)
    saves = [pltpu.make_async_copy(f_done, f_out, out_sem.at[0])]
    saves[0].start()
    p_total = nothing
    for part in range(chunks):
        where = pl.ds(part * part_rows, part_rows)
        number = 3 * chunks + part
        if number + depth < 4 * chunks:
            wave(number + depth)
        arrived(number)
        to_later(part).wait_recv()
        p_total = over_tiles(part * part_tiles, part_tiles, finish_backward, p_total)
        if part == chunks - 1:
            share(2, p_total)
        for side, (source, target) in enumerate(((b_raw, b_out), (p_raw, p_out))):
            save = pltpu.make_async_copy(
                source.at[:, where], target.at[:, where], out_sem.at[1 + 2 * part + side]
            )
            save.start()
            saves.append(save)
    for number in range(4 * chunks - depth, 4 * chunks):
        sent(number)
    for part in range(chunks):
        to_later(part).wait_send()
    means_out[2] = shared(2)
    for save in saves:
        save.wait()


def write_out(means, f_raw, b_raw, p_raw, f_out, b_out, p_out, logs_out, p_in, in_sem, out_sem):
    rows = p_in.shape[1]
    chunks = min(CHUNKS, rows // TILE)
    part_rows = rows // chunks
    views = [pl.ds(part * part_rows, part_rows) for part in range(chunks)]
    reads = [
        pltpu.make_async_copy(p_raw.at[:, where], p_in.at[:, where], in_sem.at[part])
        for part, where in enumerate(views)
    ]
    for read in reads:
        read.start()
    saves = [
        pltpu.make_async_copy(f_raw, f_out, out_sem.at[chunks]),
        pltpu.make_async_copy(b_raw, b_out, out_sem.at[chunks + 1]),
    ]
    for save in saves:
        save.start()
    scale = jnp.float32(1.0) / means[2]
    for part, where in enumerate(views):
        reads[part].wait()

        def step(tile, carry, part=part):
            start = pl.multiple_of(part * part_rows + tile * TILE, TILE)
            spot = pl.ds(start, TILE)
            p_in[:, spot, :] = p_in[:, spot, :] * scale
            return carry

        lax.fori_loop(0, part_rows // TILE, step, 0)
        save = pltpu.make_async_copy(p_in.at[:, where], p_out.at[:, where], out_sem.at[part])
        save.start()
        saves.append(save)
    which = lax.broadcasted_iota(jnp.int32, (1, 2), 1)
    logs_out[...] = jnp.log(jnp.where(which == 0, means[0], means[1]))
    for save in saves:
        save.wait()


def messages(groups, segs, forward, backward, masks, index):
    rows = forward.shape[0] // (groups * LANES)
    shape = (groups, rows, LANES)
    chunks = min(CHUNKS, rows // TILE)
    block = pltpu.VMEM(shape, jnp.float32)
    dma = pltpu.SemaphoreType.DMA
    whole = jax.ShapeDtypeStruct(shape, jnp.float32)
    anywhere = pl.BlockSpec(memory_space=pl.ANY)
    scalars = pl.BlockSpec(memory_space=pltpu.SMEM)
    hbm = pl.BlockSpec(memory_space=pltpu.HBM)
    size = forward.shape[0]
    *raw, means = pl.pallas_call(
        functools.partial(kernel, groups, segs, rows),
        out_shape=(whole, whole, whole, jax.ShapeDtypeStruct((3,), jnp.float32)),
        in_specs=[hbm] * 4,
        out_specs=(anywhere, anywhere, anywhere, scalars),
        scratch_shapes=[
            pltpu.SMEM(masks.shape, jnp.int32),
            pltpu.SMEM(index.shape, jnp.int32),
        ]
        + [block] * 15
        + [
            pltpu.VMEM((2, 3 * LANES, LANES), jnp.bfloat16),
            pltpu.VMEM((2, 2, rows, rows), jnp.bfloat16),
            pltpu.VMEM((2, rows, LANES), jnp.float32),
            pltpu.VMEM((3, TILE, LANES), jnp.float32),
            pltpu.VMEM((3, groups, TILE, LANES), jnp.float32),
            dma((4,)),
            dma((4,)),
            dma((1 + 2 * chunks,)),
            dma((4 * chunks,)),
            dma((4 * chunks,)),
            dma((chunks,)),
            dma((chunks,)),
            dma((3,)),
            dma((3,)),
        ],
        compiler_params=pltpu.CompilerParams(
            collective_id=0, has_side_effects=True, vmem_limit_bytes=44 * 1024 * 1024
        ),
        cost_estimate=pl.CostEstimate(
            flops=8 * size * (LANES + rows), bytes_accessed=20 * size, transcendentals=0
        ),
    )(masks, index, forward.reshape(shape), backward.reshape(shape))
    *outs, logs = pl.pallas_call(
        write_out,
        out_shape=(whole, whole, whole, jax.ShapeDtypeStruct((1, 2), jnp.float32)),
        in_specs=[scalars] + [anywhere] * 3,
        out_specs=(hbm, hbm, hbm, pl.BlockSpec(memory_space=pltpu.VMEM)),
        scratch_shapes=[block, dma((chunks,)), dma((chunks + 2,))],
        compiler_params=pltpu.CompilerParams(vmem_limit_bytes=8 * 1024 * 1024),
        cost_estimate=pl.CostEstimate(flops=size, bytes_accessed=24 * size, transcendentals=2),
    )(means, *raw)
    return (*(out.reshape(1, -1) for out in outs), logs.reshape(2, 1))


def shards(forward_in, backward_in, compat_masks, theta_index):
    groups = lax.axis_size("state")
    segs = lax.axis_size("seg")
    return messages(groups, segs, forward_in[0], backward_in[0], compat_masks, theta_index)


def solution(mesh):
    placed = (P("seg", "state"), P("seg", "state"), P("seg", None), P("seg", None))
    return jax.shard_map(
        shards,
        mesh=mesh,
        in_specs=placed,
        out_specs=(P("seg", "state"), P("seg", "state"), P("seg", "state"), P(None, "seg")),
        check_vma=False,
    )
```

```python
import functools

import jax
import jax.numpy as jnp
from jax import lax
from jax.experimental import pallas as pl
from jax.experimental.pallas import tpu as pltpu
from jax.sharding import PartitionSpec as P

PENALTY = 0.5
ERROR_RATE = 0.02
BASE_THETA = 0.01
LANES = 128
TILE = 8
CHUNKS = 4
DEPTH = 3
MESH = pl.DeviceIdType.MESH


def bits_of(size):
    return size.bit_length() - 1


def kernel(
    groups,
    segs,
    rows,
    masks_hbm,
    index_hbm,
    f_hbm,
    b_hbm,
    f_out,
    b_out,
    p_out,
    means_out,
    masks,
    index,
    f_in,
    b_in,
    f_send,
    f_mid,
    f_back,
    f_last,
    b_send,
    b_mid,
    b_back,
    b_last,
    f_raw,
    b_raw,
    p_raw,
    left,
    f_done,
    f_half,
    b_half,
    f_half2,
    b_half2,
    lane_mats,
    row_mats,
    tables,
    part_src,
    parts,
    load_sem,
    own_sem,
    out_sem,
    send_sem,
    recv_sem,
    seg_send,
    seg_recv,
    part_send,
    part_recv,
    near_send,
    near_recv,
    near_own,
):
    me = lax.axis_index("state")
    seg = lax.axis_index("seg")
    later = lax.rem(seg + 1, segs)
    earlier = lax.rem(seg + segs - 1, segs)
    group_bits = bits_of(groups)
    lane_bits = bits_of(LANES)
    row_bits = bits_of(rows)
    swap_first = lane_bits + row_bits
    high_first = swap_first + group_bits
    chunks = min(CHUNKS, rows // TILE)
    depth = min(DEPTH, chunks)
    part_rows = rows // chunks
    total_states = groups * groups * rows * LANES

    near = 2 ** (group_bits // 2)
    far = groups // near
    my_far = lax.div(me, near)
    my_near = lax.rem(me, near)
    first_turn = lax.rem(me * (groups // 2 - 1), groups - 1)

    def partner(step):
        turn = lax.rem(first_turn + step, groups - 1)
        odd = lax.rem(turn, 2)
        offset = (1 - odd) * (groups // 2 + lax.div(turn, 2)) + odd * lax.div(turn + 1, 2)
        other = 0
        for bit in range(group_bits):
            mine = lax.div(me, 2**bit)
            its = lax.div(offset, 2**bit)
            other = other + lax.rem(mine + its, 2) * 2**bit
        return other

    def each_partner(body):
        def step(turn, carry):
            body(partner(turn))
            return carry

        lax.fori_loop(0, groups - 1, step, 0)

    load_f = pltpu.make_async_copy(f_hbm, f_in, load_sem.at[0])
    load_b = pltpu.make_async_copy(b_hbm, b_in, load_sem.at[1])
    load_index = pltpu.make_async_copy(index_hbm, index, load_sem.at[2])
    load_masks = pltpu.make_async_copy(masks_hbm, masks, load_sem.at[3])
    load_index.start()
    load_f.start()
    load_masks.start()
    load_b.start()

    barrier = pltpu.get_barrier_semaphore()

    def greet(other):
        pl.semaphore_signal(barrier, inc=1, device_id={"state": other}, device_id_type=MESH)

    each_partner(greet)
    pl.semaphore_signal(barrier, inc=1, device_id={"seg": later}, device_id_type=MESH)
    pl.semaphore_signal(barrier, inc=1, device_id={"seg": earlier}, device_id_type=MESH)

    def theta(marker, bit):
        return lax.shift_left(jnp.int32(1), index[marker, bit]).astype(jnp.float32) * BASE_THETA

    def anchors(marker, bit):
        mask = masks[marker, bit]
        zero = jnp.where(lax.rem(mask, 2) == 1, 1.0, PENALTY).astype(jnp.float32)
        one = jnp.where(lax.div(mask, 2) == 1, 1.0, PENALTY).astype(jnp.float32)
        return zero, one

    def own_factor(marker, first):
        factor = jnp.float32(1.0)
        for bit in range(group_bits):
            zero, one = anchors(marker, first + bit)
            factor = factor * jnp.where(lax.rem(lax.div(me, 2**bit), 2) == 1, one, zero)
        return factor

    def group_factors(marker, first, own):
        factors = [own]
        for bit in range(group_bits):
            zero, one = anchors(marker, first + bit)
            factors = [f * zero for f in factors] + [f * one for f in factors]
        return factors

    def thetas(marker, first):
        return [theta(marker, first + bit) for bit in range(group_bits)]

    def mixed(values, mixing):
        values = list(values)
        for bit, amount in enumerate(mixing):
            for low in range(groups):
                high = low + 2**bit
                if low // 2**bit % 2 == 0:
                    moved = amount * (values[high] - values[low])
                    values[low] = values[low] + moved
                    values[high] = values[high] - moved
        return values

    def emitted(values, table, factors):
        return [
            v * (ERROR_RATE + (1.0 - ERROR_RATE) * (factor * table))
            for v, factor in zip(values, factors)
        ]

    def over_tiles(first, count, body, init):
        def step(which, carry):
            start = pl.multiple_of((first + which) * TILE, TILE)
            return body(pl.ds(start, TILE), carry)

        return lax.fori_loop(0, count, step, init)

    def loaded(ref, where):
        return [ref[group, where, :] for group in range(groups)]

    def stored(ref, where, values):
        for group in range(groups):
            ref[group, where, :] = values[group]

    swaps = (
        (f_send, f_half, f_mid),
        (b_send, b_half, b_mid),
        (f_back, f_half2, f_last),
        (b_back, b_half2, b_last),
    )
    own_copies = {}
    planes = set()
    here = set()

    def wave_rows(number):
        return pl.ds(number % chunks * part_rows, part_rows)

    def wave_wait(number, side, sems, blocks):
        view = swaps[number // chunks][side].at[pl.ds(0, blocks), wave_rows(number)]
        pltpu.make_async_copy(view, view, sems.at[number]).wait()

    far_blocks = (far - 1) * near
    near_blocks = (near - 1) * far

    def sent(number):
        wave_wait(number, 0, send_sem, far_blocks)
        wave_wait(number, 1, near_send, near_blocks)

    def plane(number):
        if number in planes:
            return
        planes.add(number)
        swap = number // chunks
        if swap in own_copies:
            own_copies.pop(swap).wait()
        source, target = swaps[swap][1:]
        where = wave_rows(number)
        wave_wait(number, 1, recv_sem, far_blocks)

        def send(step, carry):
            row = lax.div(step, near - 1)
            other = lax.rem(my_near + 1 + lax.rem(step, near - 1), near)
            pltpu.make_async_remote_copy(
                src_ref=source.at[row * near + other, where],
                dst_ref=target.at[row * near + my_near, where],
                send_sem=near_send.at[number],
                recv_sem=near_recv.at[number],
                device_id={"state": my_far * near + other},
                device_id_type=MESH,
            ).start()
            return carry

        lax.fori_loop(0, near_blocks, send, 0)

        def keep(row, carry):
            spot = row * near + my_near
            pltpu.make_async_copy(
                source.at[spot, where], target.at[spot, where], near_own.at[number]
            ).start()
            return carry

        lax.fori_loop(0, far, keep, 0)

    def arrived(number):
        if number in here:
            return
        here.add(number)
        plane(number)
        wave_wait(number, 2, near_own, far)
        wave_wait(number, 2, near_recv, near_blocks)

    def wave(number):
        source, target, _ = swaps[number // chunks]
        where = wave_rows(number)
        if number >= depth:
            plane(number - depth)
        if number >= 2 * depth:
            sent(number - 2 * depth)

        def send(step, carry):
            other = lax.rem(my_far + 1 + step, far)
            pltpu.make_async_remote_copy(
                src_ref=source.at[pl.ds(other * near, near), where],
                dst_ref=target.at[pl.ds(my_far * near, near), where],
                send_sem=send_sem.at[number],
                recv_sem=recv_sem.at[number],
                device_id={"state": other * near + my_near},
                device_id_type=MESH,
            ).start()
            return carry

        lax.fori_loop(0, far - 1, send, 0)

    def own_copy(swap):
        where = pl.ds(my_far * near, near)
        source, target, _ = swaps[swap]
        own_copies[swap] = pltpu.make_async_copy(
            source.at[where], target.at[where], own_sem.at[swap]
        )
        own_copies[swap].start()

    def share(which, partial):
        part_src[which] = partial
        parts[which, me] = partial

        def send(other):
            pltpu.make_async_remote_copy(
                src_ref=part_src.at[which],
                dst_ref=parts.at[which, me],
                send_sem=part_send.at[which],
                recv_sem=part_recv.at[which],
                device_id={"state": other},
                device_id_type=MESH,
            ).start()

        each_partner(send)

    def shared(which):
        view = parts.at[which, pl.ds(0, groups - 1)]
        pltpu.make_async_copy(view, view, part_send.at[which]).wait()
        pltpu.make_async_copy(view, view, part_recv.at[which]).wait()
        return jnp.sum(jnp.sum(parts[which], axis=0)) / total_states

    def kron(marker, first, count):
        width = 2**count
        differs = lax.broadcasted_iota(jnp.int32, (width, width), 0) ^ lax.broadcasted_iota(
            jnp.int32, (width, width), 1
        )
        result = jnp.ones((width, width), jnp.float32)
        for bit in range(count):
            amount = theta(marker, first + bit)
            result = result * jnp.where((differs >> bit) & 1 == 0, 1.0 - amount, amount)
        return result

    def low_table(marker):
        lane = lax.broadcasted_iota(jnp.int32, (rows, LANES), 1)
        row = lax.broadcasted_iota(jnp.int32, (rows, LANES), 0)
        result = jnp.ones((rows, LANES), jnp.float32)
        for bit in range(swap_first):
            zero, one = anchors(marker, bit)
            spot = lane >> bit if bit < lane_bits else row >> (bit - lane_bits)
            result = result * jnp.where(spot & 1 == 1, one, zero)
        return result

    tiles = rows // TILE
    part_tiles = tiles // chunks
    nothing = jnp.zeros((TILE, LANES), jnp.float32)

    load_index.wait()
    first_swap = thetas(0, swap_first)
    load_f.wait()

    def start_forward(where, carry):
        stored(f_send, where, mixed(loaded(f_in, where), first_swap))
        return carry

    for part in range(chunks):
        over_tiles(part * part_tiles, part_tiles, start_forward, 0)
        if part == 0:
            pl.semaphore_wait(barrier, groups + 1)
        if part < depth:
            wave(part)
    own_copy(0)

    load_masks.wait()
    tables[1] = low_table(1)
    load_b.wait()
    last_swap = thetas(1, swap_first)
    last_factors = group_factors(1, swap_first, own_factor(1, high_first))

    def start_backward(where, carry):
        values = emitted(loaded(b_in, where), tables[1, where, :], last_factors)
        stored(b_send, where, mixed(values, last_swap))
        return carry

    over_tiles(0, tiles, start_backward, 0)

    def halves(value):
        main = value.astype(jnp.bfloat16)
        return main, (value - main.astype(jnp.float32)).astype(jnp.bfloat16)

    def product(a, b):
        return jnp.dot(a, b, preferred_element_type=jnp.float32)

    for marker in range(2):
        main, rest = halves(kron(marker, 0, lane_bits))
        lane_mats[marker, :LANES] = main
        lane_mats[marker, LANES : 2 * LANES] = main
        lane_mats[marker, 2 * LANES :] = rest
        main, rest = halves(kron(marker, lane_bits, row_bits))
        row_mats[marker, 0] = main
        row_mats[marker, 1] = rest

    def low_mix(source, target, marker):
        def step(pair, carry):
            for which in range(2):
                group = 2 * pair + which
                main, rest = halves(source[group])
                value = product(
                    jnp.concatenate([main, rest], axis=1), lane_mats[marker, : 2 * LANES]
                ) + product(main, lane_mats[marker, 2 * LANES :])
                main, rest = halves(value)
                both = product(row_mats[marker, 0], jnp.concatenate([main, rest], axis=1))
                target[group] = (
                    both[:, :LANES] + both[:, LANES:] + product(row_mats[marker, 1], main)
                )
            return carry

        lax.fori_loop(0, groups // 2, step, 0)

    low_mix(b_send, b_send, 1)
    own_copy(1)
    tables[0] = low_table(0)
    high_mix = [thetas(0, high_first), thetas(1, high_first)]
    high_factors = group_factors(0, high_first, own_factor(0, swap_first))

    def middle(mid, before, after):
        def step(where, total):
            values = mixed(loaded(mid, where), high_mix[before])
            values = emitted(values, tables[0, where, :], high_factors)
            stored(mid, where, mixed(values, high_mix[after]))
            return total + sum(values[1:], values[0])

        return over_tiles(0, tiles, step, nothing)

    for number in range(depth, chunks + depth):
        wave(number)
    for number in range(chunks):
        arrived(number)
    low_mix(f_mid, f_mid, 0)
    middle(f_mid, 0, 1)
    low_mix(f_mid, f_back, 1)
    own_copy(2)

    for number in range(chunks + depth, 2 * chunks + depth):
        wave(number)
    for number in range(chunks, 2 * chunks):
        arrived(number)
    b_total = middle(b_mid, 1, 0)
    low_mix(b_mid, b_back, 0)
    own_copy(3)
    share(1, b_total)

    def to_later(part):
        where = pl.ds(part * part_rows, part_rows)
        return pltpu.make_async_remote_copy(
            src_ref=f_raw.at[:, where],
            dst_ref=left.at[:, where],
            send_sem=seg_send.at[part],
            recv_sem=seg_recv.at[part],
            device_id={"seg": later},
            device_id_type=MESH,
        )

    def finish_forward(where, total):
        values = emitted(
            mixed(loaded(f_last, where), last_swap), tables[1, where, :], last_factors
        )
        stored(f_raw, where, values)
        return total + sum(values[1:], values[0])

    f_total = nothing
    for part in range(chunks):
        number = 2 * chunks + part
        if number + depth < 4 * chunks:
            wave(number + depth)
        arrived(number)
        f_total = over_tiles(part * part_tiles, part_tiles, finish_forward, f_total)
        to_later(part).start()
    share(0, f_total)
    means = [shared(0), shared(1)]
    means_out[0] = means[0]
    means_out[1] = means[1]
    f_scale = jnp.float32(1.0) / means[0]
    b_scale = jnp.float32(1.0) / means[1]

    def scale_forward(where, carry):
        stored(f_done, where, [value * f_scale for value in loaded(f_raw, where)])
        return carry

    def finish_backward(where, total):
        values = mixed(loaded(b_last, where), first_swap)
        for group in range(groups):
            value = values[group] * b_scale
            b_raw[group, where, :] = value
            beside = jnp.where(seg == 0, f_in[group, where, :], left[group, where, :])
            joint = beside * value
            p_raw[group, where, :] = joint
            total = total + joint
        return total

    over_tiles(0, tiles, scale_forward, 0)
    saves = [pltpu.make_async_copy(f_done, f_out, out_sem.at[0])]
    saves[0].start()
    p_total = nothing
    for part in range(chunks):
        where = pl.ds(part * part_rows, part_rows)
        number = 3 * chunks + part
        if number + depth < 4 * chunks:
            wave(number + depth)
        arrived(number)
        to_later(part).wait_recv()
        p_total = over_tiles(part * part_tiles, part_tiles, finish_backward, p_total)
        if part == chunks - 1:
            share(2, p_total)
        for side, (source, target) in enumerate(((b_raw, b_out), (p_raw, p_out))):
            save = pltpu.make_async_copy(
                source.at[:, where], target.at[:, where], out_sem.at[1 + 2 * part + side]
            )
            save.start()
            saves.append(save)
    for number in range(4 * chunks - 2 * depth, 4 * chunks):
        sent(number)
    for part in range(chunks):
        to_later(part).wait_send()
    means_out[2] = shared(2)
    for save in saves:
        save.wait()


def write_out(means, f_raw, b_raw, p_raw, f_out, b_out, p_out, logs_out, p_in, in_sem, out_sem):
    rows = p_in.shape[1]
    chunks = min(CHUNKS, rows // TILE)
    part_rows = rows // chunks
    views = [pl.ds(part * part_rows, part_rows) for part in range(chunks)]
    reads = [
        pltpu.make_async_copy(p_raw.at[:, where], p_in.at[:, where], in_sem.at[part])
        for part, where in enumerate(views)
    ]
    for read in reads:
        read.start()
    saves = [
        pltpu.make_async_copy(f_raw, f_out, out_sem.at[chunks]),
        pltpu.make_async_copy(b_raw, b_out, out_sem.at[chunks + 1]),
    ]
    for save in saves:
        save.start()
    scale = jnp.float32(1.0) / means[2]
    for part, where in enumerate(views):
        reads[part].wait()

        def step(tile, carry, part=part):
            start = pl.multiple_of(part * part_rows + tile * TILE, TILE)
            spot = pl.ds(start, TILE)
            p_in[:, spot, :] = p_in[:, spot, :] * scale
            return carry

        lax.fori_loop(0, part_rows // TILE, step, 0)
        save = pltpu.make_async_copy(p_in.at[:, where], p_out.at[:, where], out_sem.at[part])
        save.start()
        saves.append(save)
    which = lax.broadcasted_iota(jnp.int32, (1, 2), 1)
    logs_out[...] = jnp.log(jnp.where(which == 0, means[0], means[1]))
    for save in saves:
        save.wait()


def messages(groups, segs, forward, backward, masks, index):
    rows = forward.shape[0] // (groups * LANES)
    shape = (groups, rows, LANES)
    chunks = min(CHUNKS, rows // TILE)
    block = pltpu.VMEM(shape, jnp.float32)
    dma = pltpu.SemaphoreType.DMA
    whole = jax.ShapeDtypeStruct(shape, jnp.float32)
    anywhere = pl.BlockSpec(memory_space=pl.ANY)
    scalars = pl.BlockSpec(memory_space=pltpu.SMEM)
    hbm = pl.BlockSpec(memory_space=pltpu.HBM)
    size = forward.shape[0]
    *raw, means = pl.pallas_call(
        functools.partial(kernel, groups, segs, rows),
        out_shape=(whole, whole, whole, jax.ShapeDtypeStruct((3,), jnp.float32)),
        in_specs=[hbm] * 4,
        out_specs=(anywhere, anywhere, anywhere, scalars),
        scratch_shapes=[
            pltpu.SMEM(masks.shape, jnp.int32),
            pltpu.SMEM(index.shape, jnp.int32),
        ]
        + [block] * 19
        + [
            pltpu.VMEM((2, 3 * LANES, LANES), jnp.bfloat16),
            pltpu.VMEM((2, 2, rows, rows), jnp.bfloat16),
            pltpu.VMEM((2, rows, LANES), jnp.float32),
            pltpu.VMEM((3, TILE, LANES), jnp.float32),
            pltpu.VMEM((3, groups, TILE, LANES), jnp.float32),
            dma((4,)),
            dma((4,)),
            dma((1 + 2 * chunks,)),
            dma((4 * chunks,)),
            dma((4 * chunks,)),
            dma((chunks,)),
            dma((chunks,)),
            dma((3,)),
            dma((3,)),
            dma((4 * chunks,)),
            dma((4 * chunks,)),
            dma((4 * chunks,)),
        ],
        compiler_params=pltpu.CompilerParams(
            collective_id=0, has_side_effects=True, vmem_limit_bytes=48 * 1024 * 1024
        ),
        cost_estimate=pl.CostEstimate(
            flops=8 * size * (LANES + rows), bytes_accessed=20 * size, transcendentals=0
        ),
    )(masks, index, forward.reshape(shape), backward.reshape(shape))
    *outs, logs = pl.pallas_call(
        write_out,
        out_shape=(whole, whole, whole, jax.ShapeDtypeStruct((1, 2), jnp.float32)),
        in_specs=[scalars] + [anywhere] * 3,
        out_specs=(hbm, hbm, hbm, pl.BlockSpec(memory_space=pltpu.VMEM)),
        scratch_shapes=[block, dma((chunks,)), dma((chunks + 2,))],
        compiler_params=pltpu.CompilerParams(vmem_limit_bytes=8 * 1024 * 1024),
        cost_estimate=pl.CostEstimate(flops=size, bytes_accessed=24 * size, transcendentals=2),
    )(means, *raw)
    return (*(out.reshape(1, -1) for out in outs), logs.reshape(2, 1))


def shards(forward_in, backward_in, compat_masks, theta_index):
    groups = lax.axis_size("state")
    segs = lax.axis_size("seg")
    return messages(groups, segs, forward_in[0], backward_in[0], compat_masks, theta_index)


def solution(mesh):
    placed = (P("seg", "state"), P("seg", "state"), P("seg", None), P("seg", None))
    return jax.shard_map(
        shards,
        mesh=mesh,
        in_specs=placed,
        out_specs=(P("seg", "state"), P("seg", "state"), P("seg", "state"), P(None, "seg")),
        check_vma=False,
    )
```

```python
import functools

import jax
import jax.numpy as jnp
from jax import lax
from jax.experimental import pallas as pl
from jax.experimental.pallas import tpu as pltpu
from jax.sharding import PartitionSpec as P

PENALTY = 0.5
ERROR_RATE = 0.02
BASE_THETA = 0.01
LANES = 128
TILE = 8
CHUNKS = 4
DEPTH = 4
MESH = pl.DeviceIdType.MESH


def bits_of(size):
    return size.bit_length() - 1


def kernel(
    groups,
    segs,
    rows,
    masks_hbm,
    index_hbm,
    f_hbm,
    b_hbm,
    f_out,
    b_out,
    p_out,
    means_out,
    masks,
    index,
    f_in,
    b_in,
    f_send,
    f_mid,
    f_back,
    f_last,
    b_send,
    b_mid,
    b_back,
    b_last,
    f_raw,
    b_raw,
    p_raw,
    left,
    f_done,
    lane_mats,
    row_mats,
    tables,
    part_src,
    parts,
    load_sem,
    own_sem,
    out_sem,
    send_sem,
    recv_sem,
    seg_send,
    seg_recv,
    part_send,
    part_recv,
):
    me = lax.axis_index("state")
    seg = lax.axis_index("seg")
    later = lax.rem(seg + 1, segs)
    earlier = lax.rem(seg + segs - 1, segs)
    group_bits = bits_of(groups)
    lane_bits = bits_of(LANES)
    row_bits = bits_of(rows)
    swap_first = lane_bits + row_bits
    high_first = swap_first + group_bits
    chunks = min(CHUNKS, rows // TILE)
    depth = min(DEPTH, chunks)
    part_rows = rows // chunks
    total_states = groups * groups * rows * LANES

    first_turn = lax.rem(me * (groups // 2 - 1), groups - 1)

    def partner(step):
        turn = lax.rem(first_turn + step, groups - 1)
        odd = lax.rem(turn, 2)
        offset = (1 - odd) * (groups // 2 + lax.div(turn, 2)) + odd * lax.div(turn + 1, 2)
        other = 0
        for bit in range(group_bits):
            mine = lax.div(me, 2**bit)
            its = lax.div(offset, 2**bit)
            other = other + lax.rem(mine + its, 2) * 2**bit
        return other

    def each_partner(body):
        def step(turn, carry):
            body(partner(turn))
            return carry

        lax.fori_loop(0, groups - 1, step, 0)

    load_f = pltpu.make_async_copy(f_hbm, f_in, load_sem.at[0])
    load_b = pltpu.make_async_copy(b_hbm, b_in, load_sem.at[1])
    load_index = pltpu.make_async_copy(index_hbm, index, load_sem.at[2])
    load_masks = pltpu.make_async_copy(masks_hbm, masks, load_sem.at[3])
    load_index.start()
    load_f.start()
    load_masks.start()
    load_b.start()

    barrier = pltpu.get_barrier_semaphore()

    def greet(other):
        pl.semaphore_signal(barrier, inc=1, device_id={"state": other}, device_id_type=MESH)

    each_partner(greet)
    pl.semaphore_signal(barrier, inc=1, device_id={"seg": later}, device_id_type=MESH)
    pl.semaphore_signal(barrier, inc=1, device_id={"seg": earlier}, device_id_type=MESH)

    def theta(marker, bit):
        return lax.shift_left(jnp.int32(1), index[marker, bit]).astype(jnp.float32) * BASE_THETA

    def anchors(marker, bit):
        mask = masks[marker, bit]
        zero = jnp.where(lax.rem(mask, 2) == 1, 1.0, PENALTY).astype(jnp.float32)
        one = jnp.where(lax.div(mask, 2) == 1, 1.0, PENALTY).astype(jnp.float32)
        return zero, one

    def own_factor(marker, first):
        factor = jnp.float32(1.0)
        for bit in range(group_bits):
            zero, one = anchors(marker, first + bit)
            factor = factor * jnp.where(lax.rem(lax.div(me, 2**bit), 2) == 1, one, zero)
        return factor

    def group_factors(marker, first, own):
        factors = [own]
        for bit in range(group_bits):
            zero, one = anchors(marker, first + bit)
            factors = [f * zero for f in factors] + [f * one for f in factors]
        return factors

    def thetas(marker, first):
        return [theta(marker, first + bit) for bit in range(group_bits)]

    def mixed(values, mixing):
        values = list(values)
        for bit, amount in enumerate(mixing):
            for low in range(groups):
                high = low + 2**bit
                if low // 2**bit % 2 == 0:
                    moved = amount * (values[high] - values[low])
                    values[low] = values[low] + moved
                    values[high] = values[high] - moved
        return values

    def emitted(values, table, factors):
        return [
            v * (ERROR_RATE + (1.0 - ERROR_RATE) * (factor * table))
            for v, factor in zip(values, factors)
        ]

    def over_tiles(first, count, body, init):
        def step(which, carry):
            start = pl.multiple_of((first + which) * TILE, TILE)
            return body(pl.ds(start, TILE), carry)

        return lax.fori_loop(0, count, step, init)

    def loaded(ref, where):
        return [ref[group, where, :] for group in range(groups)]

    def stored(ref, where, values):
        for group in range(groups):
            ref[group, where, :] = values[group]

    swaps = ((f_send, f_mid), (b_send, b_mid), (f_back, f_last), (b_back, b_last))

    def wave_rows(number):
        return pl.ds(number % chunks * part_rows, part_rows)

    def wave_wait(number, side, sems):
        view = swaps[number // chunks][side].at[pl.ds(0, groups - 1), wave_rows(number)]
        pltpu.make_async_copy(view, view, sems.at[number]).wait()

    def sent(number):
        wave_wait(number, 0, send_sem)

    def arrived(number):
        wave_wait(number, 1, recv_sem)

    def wave(number):
        source, target = swaps[number // chunks]
        where = wave_rows(number)
        if number >= depth:
            sent(number - depth)

        def send(other):
            pltpu.make_async_remote_copy(
                src_ref=source.at[other, where],
                dst_ref=target.at[me, where],
                send_sem=send_sem.at[number],
                recv_sem=recv_sem.at[number],
                device_id={"state": other},
                device_id_type=MESH,
            ).start()

        each_partner(send)

    def own_copy(number, source, target):
        return pltpu.make_async_copy(source.at[me], target.at[me], own_sem.at[number])

    def share(which, partial):
        part_src[which] = partial
        parts[which, me] = partial

        def send(other):
            pltpu.make_async_remote_copy(
                src_ref=part_src.at[which],
                dst_ref=parts.at[which, me],
                send_sem=part_send.at[which],
                recv_sem=part_recv.at[which],
                device_id={"state": other},
                device_id_type=MESH,
            ).start()

        each_partner(send)

    def shared(which):
        view = parts.at[which, pl.ds(0, groups - 1)]
        pltpu.make_async_copy(view, view, part_send.at[which]).wait()
        pltpu.make_async_copy(view, view, part_recv.at[which]).wait()
        return jnp.sum(jnp.sum(parts[which], axis=0)) / total_states

    def kron(marker, first, count):
        width = 2**count
        differs = lax.broadcasted_iota(jnp.int32, (width, width), 0) ^ lax.broadcasted_iota(
            jnp.int32, (width, width), 1
        )
        result = jnp.ones((width, width), jnp.float32)
        for bit in range(count):
            amount = theta(marker, first + bit)
            result = result * jnp.where((differs >> bit) & 1 == 0, 1.0 - amount, amount)
        return result

    def low_table(marker):
        lane = lax.broadcasted_iota(jnp.int32, (rows, LANES), 1)
        row = lax.broadcasted_iota(jnp.int32, (rows, LANES), 0)
        result = jnp.ones((rows, LANES), jnp.float32)
        for bit in range(swap_first):
            zero, one = anchors(marker, bit)
            spot = lane >> bit if bit < lane_bits else row >> (bit - lane_bits)
            result = result * jnp.where(spot & 1 == 1, one, zero)
        return result

    tiles = rows // TILE
    part_tiles = tiles // chunks
    nothing = jnp.zeros((TILE, LANES), jnp.float32)

    load_index.wait()
    first_swap = thetas(0, swap_first)
    load_f.wait()

    def start_forward(where, carry):
        stored(f_send, where, mixed(loaded(f_in, where), first_swap))
        return carry

    for part in range(chunks):
        over_tiles(part * part_tiles, part_tiles, start_forward, 0)
        if part == 0:
            pl.semaphore_wait(barrier, groups + 1)
        if part < depth:
            wave(part)
    own_f1 = own_copy(0, f_send, f_mid)
    own_f1.start()

    load_masks.wait()
    tables[1] = low_table(1)
    load_b.wait()
    last_swap = thetas(1, swap_first)
    last_factors = group_factors(1, swap_first, own_factor(1, high_first))

    def start_backward(where, carry):
        values = emitted(loaded(b_in, where), tables[1, where, :], last_factors)
        stored(b_send, where, mixed(values, last_swap))
        return carry

    over_tiles(0, tiles, start_backward, 0)

    def halves(value):
        main = value.astype(jnp.bfloat16)
        return main, (value - main.astype(jnp.float32)).astype(jnp.bfloat16)

    def product(a, b):
        return jnp.dot(a, b, preferred_element_type=jnp.float32)

    for marker in range(2):
        main, rest = halves(kron(marker, 0, lane_bits))
        lane_mats[marker, :LANES] = main
        lane_mats[marker, LANES : 2 * LANES] = main
        lane_mats[marker, 2 * LANES :] = rest
        main, rest = halves(kron(marker, lane_bits, row_bits))
        row_mats[marker, 0] = main
        row_mats[marker, 1] = rest

    def low_mix(source, target, marker):
        def step(pair, carry):
            for which in range(2):
                group = 2 * pair + which
                main, rest = halves(source[group])
                value = product(
                    jnp.concatenate([main, rest], axis=1), lane_mats[marker, : 2 * LANES]
                ) + product(main, lane_mats[marker, 2 * LANES :])
                main, rest = halves(value)
                both = product(row_mats[marker, 0], jnp.concatenate([main, rest], axis=1))
                target[group] = (
                    both[:, :LANES] + both[:, LANES:] + product(row_mats[marker, 1], main)
                )
            return carry

        lax.fori_loop(0, groups // 2, step, 0)

    low_mix(b_send, b_send, 1)
    own_b1 = own_copy(1, b_send, b_mid)
    own_b1.start()
    tables[0] = low_table(0)
    high_mix = [thetas(0, high_first), thetas(1, high_first)]
    high_factors = group_factors(0, high_first, own_factor(0, swap_first))

    def middle(mid, before, after):
        def step(where, total):
            values = mixed(loaded(mid, where), high_mix[before])
            values = emitted(values, tables[0, where, :], high_factors)
            stored(mid, where, mixed(values, high_mix[after]))
            return total + sum(values[1:], values[0])

        return over_tiles(0, tiles, step, nothing)

    for number in range(depth, chunks + depth):
        wave(number)
    for number in range(chunks):
        arrived(number)
    own_f1.wait()
    low_mix(f_mid, f_mid, 0)
    middle(f_mid, 0, 1)
    low_mix(f_mid, f_back, 1)
    own_f2 = own_copy(2, f_back, f_last)
    own_f2.start()

    for number in range(chunks + depth, 2 * chunks + depth):
        wave(number)
    for number in range(chunks, 2 * chunks):
        arrived(number)
    own_b1.wait()
    b_total = middle(b_mid, 1, 0)
    low_mix(b_mid, b_back, 0)
    own_b2 = own_copy(3, b_back, b_last)
    own_b2.start()
    share(1, b_total)

    def to_later(part):
        where = pl.ds(part * part_rows, part_rows)

        def send(group, carry):
            pltpu.make_async_remote_copy(
                src_ref=f_raw.at[group, where],
                dst_ref=left.at[group, where],
                send_sem=seg_send.at[part],
                recv_sem=seg_recv.at[part],
                device_id={"seg": later},
                device_id_type=MESH,
            ).start()
            return carry

        lax.fori_loop(0, groups, send, 0)

    def later_wait(part, sems):
        view = left.at[:, pl.ds(part * part_rows, part_rows)]
        pltpu.make_async_copy(view, view, sems.at[part]).wait()

    def finish_forward(where, total):
        values = emitted(
            mixed(loaded(f_last, where), last_swap), tables[1, where, :], last_factors
        )
        stored(f_raw, where, values)
        return total + sum(values[1:], values[0])

    own_f2.wait()
    f_total = nothing
    for part in range(chunks):
        number = 2 * chunks + part
        if number + depth < 4 * chunks:
            wave(number + depth)
        arrived(number)
        f_total = over_tiles(part * part_tiles, part_tiles, finish_forward, f_total)
        to_later(part)
    share(0, f_total)
    own_b2.wait()
    means = [shared(0), shared(1)]
    means_out[0] = means[0]
    means_out[1] = means[1]
    f_scale = jnp.float32(1.0) / means[0]
    b_scale = jnp.float32(1.0) / means[1]

    def scale_forward(where, carry):
        stored(f_done, where, [value * f_scale for value in loaded(f_raw, where)])
        return carry

    def finish_backward(where, total):
        values = mixed(loaded(b_last, where), first_swap)
        for group in range(groups):
            value = values[group] * b_scale
            b_raw[group, where, :] = value
            beside = jnp.where(seg == 0, f_in[group, where, :], left[group, where, :])
            joint = beside * value
            p_raw[group, where, :] = joint
            total = total + joint
        return total

    over_tiles(0, tiles, scale_forward, 0)
    saves = [pltpu.make_async_copy(f_done, f_out, out_sem.at[0])]
    saves[0].start()
    p_total = nothing
    for part in range(chunks):
        where = pl.ds(part * part_rows, part_rows)
        number = 3 * chunks + part
        if number + depth < 4 * chunks:
            wave(number + depth)
        arrived(number)
        later_wait(part, seg_recv)
        p_total = over_tiles(part * part_tiles, part_tiles, finish_backward, p_total)
        if part == chunks - 1:
            share(2, p_total)
        for side, (source, target) in enumerate(((b_raw, b_out), (p_raw, p_out))):
            save = pltpu.make_async_copy(
                source.at[:, where], target.at[:, where], out_sem.at[1 + 2 * part + side]
            )
            save.start()
            saves.append(save)
    for number in range(4 * chunks - depth, 4 * chunks):
        sent(number)
    for part in range(chunks):
        later_wait(part, seg_send)
    means_out[2] = shared(2)
    for save in saves:
        save.wait()


def write_out(means, f_raw, b_raw, p_raw, f_out, b_out, p_out, logs_out, p_in, in_sem, out_sem):
    rows = p_in.shape[1]
    chunks = min(CHUNKS, rows // TILE)
    part_rows = rows // chunks
    views = [pl.ds(part * part_rows, part_rows) for part in range(chunks)]
    reads = [
        pltpu.make_async_copy(p_raw.at[:, where], p_in.at[:, where], in_sem.at[part])
        for part, where in enumerate(views)
    ]
    for read in reads:
        read.start()
    saves = [
        pltpu.make_async_copy(f_raw, f_out, out_sem.at[chunks]),
        pltpu.make_async_copy(b_raw, b_out, out_sem.at[chunks + 1]),
    ]
    for save in saves:
        save.start()
    scale = jnp.float32(1.0) / means[2]
    for part, where in enumerate(views):
        reads[part].wait()

        def step(tile, carry, part=part):
            start = pl.multiple_of(part * part_rows + tile * TILE, TILE)
            spot = pl.ds(start, TILE)
            p_in[:, spot, :] = p_in[:, spot, :] * scale
            return carry

        lax.fori_loop(0, part_rows // TILE, step, 0)
        save = pltpu.make_async_copy(p_in.at[:, where], p_out.at[:, where], out_sem.at[part])
        save.start()
        saves.append(save)
    which = lax.broadcasted_iota(jnp.int32, (1, 2), 1)
    logs_out[...] = jnp.log(jnp.where(which == 0, means[0], means[1]))
    for save in saves:
        save.wait()


def messages(groups, segs, forward, backward, masks, index):
    rows = forward.shape[0] // (groups * LANES)
    shape = (groups, rows, LANES)
    chunks = min(CHUNKS, rows // TILE)
    block = pltpu.VMEM(shape, jnp.float32)
    dma = pltpu.SemaphoreType.DMA
    whole = jax.ShapeDtypeStruct(shape, jnp.float32)
    anywhere = pl.BlockSpec(memory_space=pl.ANY)
    scalars = pl.BlockSpec(memory_space=pltpu.SMEM)
    hbm = pl.BlockSpec(memory_space=pltpu.HBM)
    size = forward.shape[0]
    *raw, means = pl.pallas_call(
        functools.partial(kernel, groups, segs, rows),
        out_shape=(whole, whole, whole, jax.ShapeDtypeStruct((3,), jnp.float32)),
        in_specs=[hbm] * 4,
        out_specs=(anywhere, anywhere, anywhere, scalars),
        scratch_shapes=[
            pltpu.SMEM(masks.shape, jnp.int32),
            pltpu.SMEM(index.shape, jnp.int32),
        ]
        + [block] * 15
        + [
            pltpu.VMEM((2, 3 * LANES, LANES), jnp.bfloat16),
            pltpu.VMEM((2, 2, rows, rows), jnp.bfloat16),
            pltpu.VMEM((2, rows, LANES), jnp.float32),
            pltpu.VMEM((3, TILE, LANES), jnp.float32),
            pltpu.VMEM((3, groups, TILE, LANES), jnp.float32),
            dma((4,)),
            dma((4,)),
            dma((1 + 2 * chunks,)),
            dma((4 * chunks,)),
            dma((4 * chunks,)),
            dma((chunks,)),
            dma((chunks,)),
            dma((3,)),
            dma((3,)),
        ],
        compiler_params=pltpu.CompilerParams(
            collective_id=0, has_side_effects=True, vmem_limit_bytes=44 * 1024 * 1024
        ),
        cost_estimate=pl.CostEstimate(
            flops=8 * size * (LANES + rows), bytes_accessed=20 * size, transcendentals=0
        ),
    )(masks, index, forward.reshape(shape), backward.reshape(shape))
    *outs, logs = pl.pallas_call(
        write_out,
        out_shape=(whole, whole, whole, jax.ShapeDtypeStruct((1, 2), jnp.float32)),
        in_specs=[scalars] + [anywhere] * 3,
        out_specs=(hbm, hbm, hbm, pl.BlockSpec(memory_space=pltpu.VMEM)),
        scratch_shapes=[block, dma((chunks,)), dma((chunks + 2,))],
        compiler_params=pltpu.CompilerParams(vmem_limit_bytes=8 * 1024 * 1024),
        cost_estimate=pl.CostEstimate(flops=size, bytes_accessed=24 * size, transcendentals=2),
    )(means, *raw)
    return (*(out.reshape(1, -1) for out in outs), logs.reshape(2, 1))


def shards(forward_in, backward_in, compat_masks, theta_index):
    groups = lax.axis_size("state")
    segs = lax.axis_size("seg")
    return messages(groups, segs, forward_in[0], backward_in[0], compat_masks, theta_index)


def solution(mesh):
    placed = (P("seg", "state"), P("seg", "state"), P("seg", None), P("seg", None))
    return jax.shard_map(
        shards,
        mesh=mesh,
        in_specs=placed,
        out_specs=(P("seg", "state"), P("seg", "state"), P("seg", "state"), P(None, "seg")),
        check_vma=False,
    )
```
